32 devices in a mesh: tm: 16 (over z, y, core), space: 2 (over x).
Axes of the slice: x: 2, y: 2, z: 4, core: 2. Of those that a mesh axis runs over, the one named last changes fastest.
Arguments:
- queries: bfloat16 [4096, 4096], P(('tm', 'space')), may hold values from -14 to 14
- keys: bfloat16 [4096, 2048], P(('tm', 'space')), may hold values from -6 to 6
- values: bfloat16 [4096, 2048], P(('tm', 'space')), may hold values from -6 to 6
- output_gradient: bfloat16 [4096, 4096], P(('tm', 'space')), may hold values from -6 to 6
- tiles: int32 [32, 6], P('tm'), may hold values from 0 to 5, as said below
- kinds: int32 [32, 6], P('tm'), may hold values from 0 to 2, as said below
Outputs:
- grad_queries: bfloat16 [4096, 4096], P(('tm', 'space'))
- grad_keys: bfloat16 [4096, 2048], P(('tm', 'space'))
- grad_values: bfloat16 [4096, 2048], P(('tm', 'space'))
The draws below stay inside these ranges and needn't reach their ends.
Inputs may be any that keep to these rules, and one draw needn't show every extreme that they name: Row b lists the key tiles of query block b, which lies in window w = b // 2 at block b % 2 of it. A value v names kv block v % 2 of window w - v // 2; windows below 0 are never named, nor, where v // 2 = 0, blocks at or after b % 2 except in slot 0. Slot 0 holds b % 2; slots 1 to u hold distinct other values, u from 0 to 5, ragged over the blocks; the remaining slots hold 0. Every draw has rows with u = 5 and names the largest value. `kinds`: kind 0: every key of the tile is visible; kind 1: a key is visible when its position in its tile is at most the query's position in its block; kind 2: the slot is unused. Slot 0 has kind 1, used slots kind 0 or 1, unused slots kind 2.
All inputs are finite; a program needn't handle non-finite values.
Results may differ from the reference program's by a relative error of at most 0.015.
Values may be sent and summed in bfloat16 or wider, within the bound.
No kernel may reach another device: no remote copies, remote signals or barrier semaphores. Data moves between devices by JAX's collectives and lax.ppermute only.
A program may use at most 128 MiB of HBM per device.

```python
import jax
import jax.numpy as jnp
from jax import lax

QUERY_HEAD_COUNT = 32
KEY_VALUE_HEADS = 16
HEAD_SIZE = 128
BLOCK_TOKENS = 128
MAXT = 6
REACH = 2
KBW = 2
SEQUENCE_TOKENS = 4096
QUERY_BLOCK_COUNT = 32


def draw_keys(key, part):
    unsigned_tiles = jnp.clip(jax.random.normal(jax.random.fold_in(key, 1), (SEQUENCE_TOKENS, KEY_VALUE_HEADS * HEAD_SIZE), jnp.float32), -6.0, 6.0)
    return unsigned_tiles.astype(jnp.bfloat16)


def draw_queries(key, part):
    unsigned_tiles = jnp.clip(jax.random.normal(jax.random.fold_in(key, 4), (SEQUENCE_TOKENS, QUERY_HEAD_COUNT * HEAD_SIZE), jnp.float32), -6.0, 6.0)
    return unsigned_tiles.astype(jnp.bfloat16)


def tile_plan(key):
    block = jnp.arange(QUERY_BLOCK_COUNT, dtype=jnp.int32)
    window = block // KBW
    own_block = block % KBW
    cells = (REACH + 1) * KBW
    candidate = jnp.arange(cells, dtype=jnp.int32)
    distance = candidate // KBW
    column = candidate % KBW
    valid = (distance[None, :] <= window[:, None]) & ((distance[None, :] > 0) | (column[None, :] < own_block[:, None]))
    last_row = (own_block == KBW - 1) & (window >= REACH)
    forced = last_row[:, None] & (candidate[None, :] == cells - 1)
    noise = jax.random.randint(jax.random.fold_in(key, 201), (QUERY_BLOCK_COUNT, cells), 0, 1 << 20, dtype=jnp.int32)
    ranking = noise * cells + candidate[None, :]
    ranking = jnp.where(valid, ranking, ranking + (1 << 30))
    ranking = jnp.where(forced, -1, ranking)
    ordered = jnp.argsort(ranking, axis=1, stable=True)[:, :MAXT - 1].astype(jnp.int32)
    valid_count = jnp.sum(valid.astype(jnp.int32), axis=1)
    wanted = jax.random.randint(jax.random.fold_in(key, 202), (QUERY_BLOCK_COUNT,), 0, MAXT, dtype=jnp.int32)
    wanted = jnp.where(last_row, MAXT - 1, wanted)
    used_count = jnp.minimum(wanted, valid_count)
    slot = jnp.arange(1, MAXT, dtype=jnp.int32)
    active = slot[None, :] <= used_count[:, None]
    extra_tiles = jnp.where(active, ordered, 0)
    extra_kinds = jax.random.randint(jax.random.fold_in(key, 203), (QUERY_BLOCK_COUNT, MAXT - 1), 0, 2, dtype=jnp.int32)
    extra_kinds = jnp.where(last_row[:, None] & (slot[None, :] == 1), 0, extra_kinds)
    extra_kinds = jnp.where(active, extra_kinds, 2)
    tile_table = jnp.concatenate([own_block[:, None], extra_tiles], axis=1).astype(jnp.int32)
    kind_table = jnp.concatenate([jnp.ones((QUERY_BLOCK_COUNT, 1), jnp.int32), extra_kinds], axis=1).astype(jnp.int32)
    return (tile_table, kind_table)


def draw_tiles(key, part):
    return tile_plan(key)[0]


def draw_kinds(key, part):
    return tile_plan(key)[1]


def block_levels(own_key, dims, shards, low, top_value):
    gain = 1.0
    for dim, shards_of in shards:
        draws = jax.random.uniform(jax.random.fold_in(jax.random.fold_in(own_key, 6), dim), (shards_of,), jnp.float32, low / len(shards), top_value / len(shards))
        gain = gain * jnp.repeat(jnp.exp(draws), dims[dim] // shards_of).reshape((-1,) + (1,) * (len(dims) - 1 - dim))
    return gain


def scatter_about(stream_key, shape, deviation, reach, split=(), held_as=jnp.bfloat16):
    values = jax.random.normal(stream_key, shape, jnp.float32) * deviation
    if len(split) > 0:
        values = block_levels(stream_key, shape, split, -0.22, 0.18) * values
    return jnp.clip(values, min=-reach, max=reach).astype(held_as)


def setup_inputs(seed: int = 0) -> dict:
    seeds = jax.random.split(jax.random.key(seed), 7)
    return {
        "queries": draw_queries(jax.random.fold_in(seeds[6], 71), 0),
        "keys": draw_keys(jax.random.fold_in(seeds[6], 71), 0),
        "values": scatter_about(seeds[2], (SEQUENCE_TOKENS, KEY_VALUE_HEADS * HEAD_SIZE), 1.0, 6.0, ((0, 32),)),
        "output_gradient": scatter_about(seeds[3], (SEQUENCE_TOKENS, QUERY_HEAD_COUNT * HEAD_SIZE), 1.0, 6.0, ((0, 32),)),
        "tiles": draw_tiles(jax.random.fold_in(seeds[6], 71), 0),
        "kinds": draw_kinds(jax.random.fold_in(seeds[6], 71), 0),
    }


def block_grads(query_rows, grad_rows, key_tiles, value_tiles, tile_kinds):
    blocks, length, kv_count, head_dim = key_tiles.shape
    score_scale = 1.0 / (head_dim ** 0.5)
    key_flat = key_tiles.reshape(blocks * length, kv_count, head_dim)
    value_flat = value_tiles.reshape(blocks * length, kv_count, head_dim)
    highest = lax.Precision.HIGHEST
    scores = jnp.einsum("qkgd,tkd->kgqt", query_rows, key_flat, precision=highest) * score_scale
    query_pos = jnp.arange(length)
    column_kind = jnp.repeat(tile_kinds, length)
    column_pos = jnp.tile(jnp.arange(length), blocks)
    visible = (column_kind == 0)[None, :] | ((column_kind == 1)[None, :] & (column_pos[None, :] <= query_pos[:, None]))
    masked = jnp.where(visible, scores, -jnp.inf)
    row_max = jnp.max(masked, axis=-1, keepdims=True)
    weights = jnp.where(visible, jnp.exp(masked - row_max), 0.0)
    probabilities = weights / jnp.sum(weights, axis=-1, keepdims=True)
    probs_low = probabilities.astype(jnp.bfloat16).astype(jnp.float32)
    outputs = jnp.einsum("kgqt,tkd->qkgd", probs_low, value_flat, precision=highest)
    row_delta = jnp.einsum("qkgd,qkgd->kgq", grad_rows, outputs, precision=highest)
    grad_probs = jnp.einsum("qkgd,tkd->kgqt", grad_rows, value_flat, precision=highest)
    grad_scores = (score_scale * probabilities * (grad_probs - row_delta[..., None])).astype(jnp.bfloat16).astype(jnp.float32)
    grad_query = jnp.einsum("kgqt,tkd->qkgd", grad_scores, key_flat, precision=highest)
    grad_key = jnp.einsum("kgqt,qkgd->tkd", grad_scores, query_rows, precision=highest)
    grad_value = jnp.einsum("kgqt,qkgd->tkd", probs_low, grad_rows, precision=highest)
    return (grad_query.astype(jnp.bfloat16),
            grad_key.reshape(blocks, length, kv_count, head_dim),
            grad_value.reshape(blocks, length, kv_count, head_dim))


def reference(queries, keys, values, output_gradient, tiles, kinds):
    head_groups = QUERY_HEAD_COUNT // KEY_VALUE_HEADS
    key_block_rows = keys.reshape(QUERY_BLOCK_COUNT, BLOCK_TOKENS, KEY_VALUE_HEADS, HEAD_SIZE)
    value_block_rows = values.reshape(QUERY_BLOCK_COUNT, BLOCK_TOKENS, KEY_VALUE_HEADS, HEAD_SIZE)
    query_block_rows = queries.reshape(QUERY_BLOCK_COUNT, BLOCK_TOKENS, KEY_VALUE_HEADS, head_groups, HEAD_SIZE)
    block_gradients = output_gradient.reshape(QUERY_BLOCK_COUNT, BLOCK_TOKENS, KEY_VALUE_HEADS, head_groups, HEAD_SIZE)

    def advance(totals, block_index):
        summed_key_grad, summed_value_grad = totals
        window = block_index // KBW
        tile_row = tiles[block_index]
        source = ((window - tile_row // KBW) * KBW + tile_row % KBW).astype(jnp.int32)
        grad_query, grad_key, grad_value = block_grads(
            query_block_rows[block_index].astype(jnp.float32),
            block_gradients[block_index].astype(jnp.float32),
            key_block_rows[source].astype(jnp.float32),
            value_block_rows[source].astype(jnp.float32),
            kinds[block_index])
        return (summed_key_grad.at[source].add(grad_key), summed_value_grad.at[source].add(grad_value)), grad_query

    blank_total_sum = jnp.zeros((QUERY_BLOCK_COUNT, BLOCK_TOKENS, KEY_VALUE_HEADS, HEAD_SIZE), jnp.float32)
    (summed_key_grad, summed_value_grad), grad_queries = lax.scan(advance, (blank_total_sum, blank_total_sum), jnp.arange(QUERY_BLOCK_COUNT, dtype=jnp.int32))
    return (grad_queries.reshape(SEQUENCE_TOKENS, QUERY_HEAD_COUNT * HEAD_SIZE),
            summed_key_grad.reshape(SEQUENCE_TOKENS, KEY_VALUE_HEADS * HEAD_SIZE).astype(jnp.bfloat16),
            summed_value_grad.reshape(SEQUENCE_TOKENS, KEY_VALUE_HEADS * HEAD_SIZE).astype(jnp.bfloat16))
```

```python
import math

import jax
import jax.numpy as jnp
from jax import lax
from jax.experimental import pallas as pl
from jax.experimental.pallas import tpu as pltpu
from jax.sharding import PartitionSpec as P

HEAD_SIZE = 128
BLOCK_TOKENS = 128
MAXT = 6
REACH = 2
CHUNKS = 2
HIDDEN = -1e30
FAR = 1 << 20


def shifted_2(block, axis, distance):
    devices = range(lax.axis_size(axis))
    route = [(i - distance, i) for i in devices if i - distance in devices]
    return lax.ppermute(block, axis, route)


def block_grads(query_rows, grad_rows, key_tiles, value_tiles, tile_kinds):
    blocks, length, kv_count, head_dim = key_tiles.shape
    score_scale = 1.0 / head_dim**0.5
    key_flat = key_tiles.reshape(blocks * length, kv_count, head_dim)
    value_flat = value_tiles.reshape(blocks * length, kv_count, head_dim)
    scores = (
        jnp.einsum("qkgd,tkd->kgqt", query_rows, key_flat, preferred_element_type=jnp.float32)
        * score_scale
    )
    query_pos = jnp.arange(length)
    column_kind = jnp.repeat(tile_kinds, length)
    column_pos = jnp.tile(jnp.arange(length), blocks)
    visible = (column_kind == 0)[None, :] | (column_kind == 1)[None, :] & (
        column_pos[None, :] <= query_pos[:, None]
    )
    masked = jnp.where(visible, scores, -jnp.inf)
    row_max = jnp.max(masked, axis=-1, keepdims=True)
    weights = jnp.where(visible, jnp.exp(masked - row_max), 0.0)
    probabilities = weights / jnp.sum(weights, axis=-1, keepdims=True)
    probs_low = probabilities.astype(jnp.bfloat16)
    outputs = jnp.einsum(
        "kgqt,tkd->qkgd", probs_low, value_flat, preferred_element_type=jnp.float32
    )
    row_delta = jnp.einsum("qkgd,qkgd->kgq", grad_rows.astype(jnp.float32), outputs)
    grad_probs = jnp.einsum(
        "qkgd,tkd->kgqt", grad_rows, value_flat, preferred_element_type=jnp.float32
    )
    grad_scores = (score_scale * probabilities * (grad_probs - row_delta[..., None])).astype(
        jnp.bfloat16
    )
    grad_query = jnp.einsum(
        "kgqt,tkd->qkgd", grad_scores, key_flat, preferred_element_type=jnp.float32
    )
    grad_key = jnp.einsum(
        "kgqt,qkgd->tkd", grad_scores, query_rows, preferred_element_type=jnp.float32
    )
    grad_value = jnp.einsum(
        "kgqt,qkgd->tkd", probs_low, grad_rows, preferred_element_type=jnp.float32
    )
    return (
        grad_query.astype(jnp.bfloat16),
        grad_key.reshape(blocks, length, kv_count, head_dim),
        grad_value.reshape(blocks, length, kv_count, head_dim),
    )


def general_body(queries, keys, values, output_gradient, tiles, kinds):
    query_heads, grad_heads, key_heads, value_heads = (
        lax.all_to_all(queries, "space", split_axis=1, concat_axis=0, tiled=True),
        lax.all_to_all(output_gradient, "space", split_axis=1, concat_axis=0, tiled=True),
        lax.all_to_all(keys, "space", split_axis=1, concat_axis=0, tiled=True),
        lax.all_to_all(values, "space", split_axis=1, concat_axis=0, tiled=True),
    )
    window = query_heads.shape[0]
    kv_heads = key_heads.shape[1] // HEAD_SIZE
    head_groups = query_heads.shape[1] // key_heads.shape[1]
    per_window = window // BLOCK_TOKENS
    earlier = [shifted_2((key_heads, value_heads), "tm", offset) for offset in range(1, REACH + 1)]
    tile_count = (REACH + 1) * per_window
    key_tiles = jnp.concatenate([key_heads] + [shifted[0] for shifted in earlier], axis=0)
    key_tiles = key_tiles.reshape(tile_count, BLOCK_TOKENS, kv_heads, HEAD_SIZE)
    value_tiles = jnp.concatenate([value_heads] + [shifted[1] for shifted in earlier], axis=0)
    value_tiles = value_tiles.reshape(tile_count, BLOCK_TOKENS, kv_heads, HEAD_SIZE)
    group_size = math.gcd(per_window, 4)
    rounds = per_window // group_size
    query_groups = query_heads.reshape(
        rounds, group_size, BLOCK_TOKENS, kv_heads, head_groups, HEAD_SIZE
    )
    grad_groups = grad_heads.reshape(
        rounds, group_size, BLOCK_TOKENS, kv_heads, head_groups, HEAD_SIZE
    )
    tile_groups = tiles.reshape(rounds, group_size, MAXT)
    kind_groups = kinds.reshape(rounds, group_size, MAXT)

    def one_round(totals, inputs):
        summed_key_grad, summed_value_grad = totals
        query_part, grad_part, tile_part, kind_part = inputs
        flat_tiles = tile_part.reshape(group_size * MAXT)
        grad_query, grad_key, grad_value = jax.vmap(block_grads)(
            query_part, grad_part, key_tiles[tile_part], value_tiles[tile_part], kind_part
        )
        summed_key_grad = summed_key_grad.at[flat_tiles].add(
            grad_key.reshape(group_size * MAXT, BLOCK_TOKENS, kv_heads, HEAD_SIZE)
        )
        summed_value_grad = summed_value_grad.at[flat_tiles].add(
            grad_value.reshape(group_size * MAXT, BLOCK_TOKENS, kv_heads, HEAD_SIZE)
        )
        return ((summed_key_grad, summed_value_grad), grad_query)

    blank_total_sum = jnp.zeros((tile_count, BLOCK_TOKENS, kv_heads, HEAD_SIZE), jnp.float32)
    (summed_key_grad, summed_value_grad), grad_queries = lax.scan(
        one_round,
        (blank_total_sum, blank_total_sum),
        (query_groups, grad_groups, tile_groups, kind_groups),
    )
    key_parts = summed_key_grad.reshape(REACH + 1, window, kv_heads * HEAD_SIZE)
    value_parts = summed_value_grad.reshape(REACH + 1, window, kv_heads * HEAD_SIZE)
    moving_sum = (key_parts[REACH], value_parts[REACH])
    for offset in range(REACH - 1, -1, -1):
        arrived = shifted_2((moving_sum[0], moving_sum[1]), "tm", -1)
        moving_sum = (arrived[0] + key_parts[offset], arrived[1] + value_parts[offset])
    key_total, value_total = moving_sum
    grad_query_heads = grad_queries.reshape(window, head_groups * kv_heads * HEAD_SIZE)
    return (
        lax.all_to_all(grad_query_heads, "space", split_axis=0, concat_axis=1, tiled=True),
        lax.all_to_all(
            key_total.astype(jnp.bfloat16), "space", split_axis=0, concat_axis=1, tiled=True
        ),
        lax.all_to_all(
            value_total.astype(jnp.bfloat16), "space", split_axis=0, concat_axis=1, tiled=True
        ),
    )


def packed(arrays, part, chunk, chunks):
    half = arrays[0].shape[1] // 2
    width = half // chunks
    first = part * half + chunk * width
    return jnp.concatenate([lax.dynamic_slice_in_dim(a, first, width, 1) for a in arrays], axis=0)


def dot(a, b, contract):
    return lax.dot_general(a, b, ((contract[:1], contract[1:]), ((), ())), preferred_element_type=jnp.float32)


def attend_kernel(
    side_ref, limit_ref,
    q_own, g_own, qg_other, k_own, v_own, kv_other, kv2_own, kv2_other, kv1,
    dq_own, dq_other, d0, d1, d2_own, d2_other,
    q_all, g_all, k_all, v_all, s_ref, dp_ref, p_ref, ds_ref,
):
    n, d = BLOCK_TOKENS, HEAD_SIZE
    for r, (q, g) in enumerate(
        ((q_own[...], g_own[...]), (qg_other[:n, :], qg_other[n:, :]))
    ):
        for j in range(2):
            rows = pl.ds((2 * r + j) * n, n)
            q_all[rows, :] = q[:, j * d : (j + 1) * d]
            g_all[rows, :] = g[:, j * d : (j + 1) * d]
    tiles = (
        (k_own[...], v_own[...]),
        (kv_other[:n, :], kv_other[n:, :]),
        (kv1[:n, :], kv1[n : 2 * n, :]),
        (kv1[2 * n : 3 * n, :], kv1[3 * n :, :]),
        (kv2_own[:n, :], kv2_own[n:, :]),
        (kv2_other[:n, :], kv2_other[n:, :]),
    )
    for p, (k, v) in enumerate(tiles):
        k_all[p * n : (p + 1) * n, :] = k
        v_all[p * n : (p + 1) * n, :] = v
    lanes = 2 * n
    column = lax.broadcasted_iota(jnp.int32, (n, lanes), 0)
    row = lax.broadcasted_iota(jnp.int32, (n, lanes), 1)
    ahead = column - jnp.where(row >= n, row - n, row)
    scale = 1.0 / math.sqrt(d)
    for r in range(2):
        q = q_all[r * lanes : (r + 1) * lanes, :]
        g = g_all[r * lanes : (r + 1) * lanes, :]
        top = None
        for p in range(6):
            s = dot(k_all[p * n : (p + 1) * n, :], q, (1, 1))
            s = jnp.where(ahead <= limit_ref[r * 6 + p], s, HIDDEN)
            s_ref[p * n : (p + 1) * n, :] = s
            high = jnp.max(s, axis=0, keepdims=True)
            top = high if top is None else jnp.maximum(top, high)
        total = jnp.zeros((1, lanes), jnp.float32)
        for p in range(6):
            e = jnp.exp((s_ref[p * n : (p + 1) * n, :] - top) * scale)
            s_ref[p * n : (p + 1) * n, :] = e
            total = total + jnp.sum(e, axis=0, keepdims=True)
        share = 1.0 / total
        delta = jnp.zeros((1, lanes), jnp.float32)
        for p in range(6):
            dp = dot(v_all[p * n : (p + 1) * n, :], g, (1, 1))
            prob = s_ref[p * n : (p + 1) * n, :] * share
            low = prob.astype(jnp.bfloat16)
            delta = delta + jnp.sum(low.astype(jnp.float32) * dp, axis=0, keepdims=True)
            s_ref[p * n : (p + 1) * n, :] = prob * scale
            dp_ref[p * n : (p + 1) * n, :] = dp
            p_ref[p * n : (p + 1) * n, r * lanes : (r + 1) * lanes] = low
        for p in range(6):
            ds = s_ref[p * n : (p + 1) * n, :] * (dp_ref[p * n : (p + 1) * n, :] - delta)
            ds_ref[p * n : (p + 1) * n, r * lanes : (r + 1) * lanes] = ds.astype(jnp.bfloat16)
    homes = ((d0, 0), (d0, 2), (d1, 0), (d1, 2), (d2_own, 0), (d2_other, 0))
    for p, (out, place) in enumerate(homes):
        dk = dot(ds_ref[p * n : (p + 1) * n, :], q_all[...], (1, 0))
        dv = dot(p_ref[p * n : (p + 1) * n, :], g_all[...], (1, 0))
        out[place * n : (place + 1) * n, :] = dk.astype(out.dtype)
        out[(place + 1) * n : (place + 2) * n, :] = dv.astype(out.dtype)
    dq = dot(k_all[...], ds_ref[...], (0, 0)).T.astype(jnp.bfloat16)
    for j in range(2):
        dq_own[:, j * d : (j + 1) * d] = dq[j * n : (j + 1) * n, :]
        dq_other[:, j * d : (j + 1) * d] = dq[(2 + j) * n : (3 + j) * n, :]


def attend(side, limits, chunk, heads, queries, grads, keys, values, qg_other, kv_other, kv2_own, kv2_other, kv1):
    n, d = BLOCK_TOKENS, HEAD_SIZE
    per_side = keys.shape[1] // (2 * d)

    def mine(h, side_ref, limit_ref):
        return 0, side_ref[0] * per_side + chunk * heads + h

    def here(h, side_ref, limit_ref):
        return 0, h

    def out(rows, width, dtype):
        return (
            jax.ShapeDtypeStruct((rows, heads * width), dtype),
            pl.BlockSpec((rows, width), here),
        )

    outs = [
        out(n, 2 * d, jnp.bfloat16),
        out(n, 2 * d, jnp.bfloat16),
        out(4 * n, d, jnp.float32),
        out(4 * n, d, jnp.bfloat16),
        out(2 * n, d, jnp.bfloat16),
        out(2 * n, d, jnp.bfloat16),
    ]
    flops = heads * 5 * 2 * 4 * n * 6 * n * d
    return pl.pallas_call(
        attend_kernel,
        grid_spec=pltpu.PrefetchScalarGridSpec(
            num_scalar_prefetch=2,
            grid=(heads,),
            in_specs=[
                pl.BlockSpec((n, 2 * d), mine),
                pl.BlockSpec((n, 2 * d), mine),
                pl.BlockSpec((2 * n, 2 * d), here),
                pl.BlockSpec((n, d), mine),
                pl.BlockSpec((n, d), mine),
                pl.BlockSpec((2 * n, d), here),
                pl.BlockSpec((2 * n, d), here),
                pl.BlockSpec((2 * n, d), here),
                pl.BlockSpec((4 * n, d), here),
            ],
            out_specs=[spec for _, spec in outs],
            scratch_shapes=[
                pltpu.VMEM((4 * n, d), jnp.bfloat16),
                pltpu.VMEM((4 * n, d), jnp.bfloat16),
                pltpu.VMEM((6 * n, d), jnp.bfloat16),
                pltpu.VMEM((6 * n, d), jnp.bfloat16),
                pltpu.VMEM((6 * n, 2 * n), jnp.float32),
                pltpu.VMEM((6 * n, 2 * n), jnp.float32),
                pltpu.VMEM((6 * n, 4 * n), jnp.bfloat16),
                pltpu.VMEM((6 * n, 4 * n), jnp.bfloat16),
            ],
        ),
        out_shape=[shape for shape, _ in outs],
        compiler_params=pltpu.CompilerParams(vmem_limit_bytes=32 * 1024 * 1024),
        cost_estimate=pl.CostEstimate(
            flops=flops, bytes_accessed=heads * 30 * n * d * 2, transcendentals=heads * 24 * n * n
        ),
    )(side, limits, queries, grads, qg_other, keys, values, kv_other, kv2_own, kv2_other, kv1)


def swap(block):
    return lax.ppermute(block, "space", [(0, 1), (1, 0)])


def mate(block):
    return lax.ppermute(block, "tm", [(i, i ^ 1) for i in range(lax.axis_size("tm"))])


def moved(block, distance):
    size = lax.axis_size("tm")
    return lax.ppermute(
        block, "tm", [(i, i + distance) for i in range(size) if 0 <= i + distance < size]
    )


def column_limits(side, tiles, kinds):
    block = jnp.stack([side, 1 - side])
    value = (jnp.arange(REACH + 1)[:, None] * 2 + block[None, :]).reshape(-1)
    tiles, kinds = tiles[block], kinds[block]
    limit = jnp.where(kinds == 0, FAR, jnp.where(kinds == 1, 0, -FAR))
    named = tiles[:, None, :] == value[None, :, None]
    return jnp.max(jnp.where(named, limit[:, None, :], -FAR), axis=2).reshape(-1).astype(jnp.int32)


def pair_body(queries, keys, values, output_gradient, tiles, kinds):
    n, d = BLOCK_TOKENS, HEAD_SIZE
    side = lax.axis_index("space")
    odd = lax.axis_index("tm") % 2 == 1
    heads = keys.shape[1] // (2 * d) // CHUNKS
    place = side.reshape(1).astype(jnp.int32)
    limits = column_limits(side, tiles, kinds)

    kv_away = [packed([keys, values], 1 - side, c, CHUNKS) for c in range(CHUNKS)]
    kv_own = [packed([keys, values], side, c, CHUNKS) for c in range(CHUNKS)]
    qg_away = [packed([queries, output_gradient], 1 - side, c, CHUNKS) for c in range(CHUNKS)]

    kv_other = [swap(b) for b in kv_away]
    qg_other = [swap(b) for b in qg_away]
    kv2_own = [moved(b, 2) for b in kv_own]
    kv2_other = [moved(b, 2) for b in kv_other]

    dq, dkv = [], []
    for c in range(CHUNKS):
        kv1 = mate(
            jnp.concatenate(
                [
                    jnp.where(odd, kv2_own[c], kv_own[c]),
                    jnp.where(odd, kv2_other[c], kv_other[c]),
                ],
                axis=0,
            )
        )
        dq_own, dq_away, d0, d1, d2_own, d2_other = attend(
            place, limits, c, heads, queries, output_gradient, keys, values,
            qg_other[c], kv_other[c], kv2_own[c], kv2_other[c], kv1,
        )
        dq_other = swap(dq_away)
        met = mate(d1).astype(jnp.float32)
        met_back = jnp.where(odd, met, 0.0)
        met_here = jnp.where(odd, 0.0, met)
        back_other = moved((d2_other + met_back[2 * n :]).astype(jnp.bfloat16), -2)
        back_own = moved((d2_own + met_back[: 2 * n]).astype(jnp.bfloat16), -2)
        sum_other = (d0[2 * n :] + met_here[2 * n :] + back_other).astype(jnp.bfloat16)
        sum_own = (d0[: 2 * n] + met_here[: 2 * n] + back_own).astype(jnp.bfloat16)
        dkv_other = swap(sum_other)
        dq.append((dq_own, dq_other))
        dkv.append((sum_own, dkv_other))

    def placed(own, other):
        own, other = jnp.concatenate(own, axis=1), jnp.concatenate(other, axis=1)
        return jnp.where(
            side == 0,
            jnp.concatenate([own, other], axis=1),
            jnp.concatenate([other, own], axis=1),
        )

    return (
        placed([a for a, _ in dq], [b for _, b in dq]),
        placed([a[:n] for a, _ in dkv], [b[:n] for _, b in dkv]),
        placed([a[n:] for a, _ in dkv], [b[n:] for _, b in dkv]),
    )


def body(queries, keys, values, output_gradient, tiles, kinds):
    pair = (
        lax.axis_size("space") == 2
        and lax.axis_size("tm") % 2 == 0
        and tiles.shape[0] == 2
        and queries.shape[0] == BLOCK_TOKENS
        and queries.shape[1] == 2 * keys.shape[1]
        and keys.shape[1] % (2 * HEAD_SIZE * CHUNKS) == 0
    )
    run = pair_body if pair else general_body
    return run(queries, keys, values, output_gradient, tiles, kinds)


def solution(mesh):
    in_specs = (
        P(("tm", "space"), None),
        P(("tm", "space"), None),
        P(("tm", "space"), None),
        P(("tm", "space"), None),
        P("tm", None),
        P("tm", None),
    )
    out_specs = (P(("tm", "space"), None), P(("tm", "space"), None), P(("tm", "space"), None))
    return jax.shard_map(body, mesh=mesh, in_specs=in_specs, out_specs=out_specs, check_vma=False)
```

```python
import math

import jax
import jax.numpy as jnp
from jax import lax
from jax.experimental import pallas as pl
from jax.experimental.pallas import tpu as pltpu
from jax.sharding import PartitionSpec as P

HEAD_SIZE = 128
BLOCK_TOKENS = 128
MAXT = 6
REACH = 2
STEP_HEADS = 1
HIDDEN = -1e30
FAR = 1 << 20
VMEM_BYTES = 60 * 1024 * 1024


def shifted_2(block, axis, distance):
    devices = range(lax.axis_size(axis))
    route = [(i - distance, i) for i in devices if i - distance in devices]
    return lax.ppermute(block, axis, route)


def block_grads(query_rows, grad_rows, key_tiles, value_tiles, tile_kinds):
    blocks, length, kv_count, head_dim = key_tiles.shape
    score_scale = 1.0 / head_dim**0.5
    key_flat = key_tiles.reshape(blocks * length, kv_count, head_dim)
    value_flat = value_tiles.reshape(blocks * length, kv_count, head_dim)
    scores = (
        jnp.einsum("qkgd,tkd->kgqt", query_rows, key_flat, preferred_element_type=jnp.float32)
        * score_scale
    )
    query_pos = jnp.arange(length)
    column_kind = jnp.repeat(tile_kinds, length)
    column_pos = jnp.tile(jnp.arange(length), blocks)
    visible = (column_kind == 0)[None, :] | (column_kind == 1)[None, :] & (
        column_pos[None, :] <= query_pos[:, None]
    )
    masked = jnp.where(visible, scores, -jnp.inf)
    row_max = jnp.max(masked, axis=-1, keepdims=True)
    weights = jnp.where(visible, jnp.exp(masked - row_max), 0.0)
    probabilities = weights / jnp.sum(weights, axis=-1, keepdims=True)
    probs_low = probabilities.astype(jnp.bfloat16)
    outputs = jnp.einsum(
        "kgqt,tkd->qkgd", probs_low, value_flat, preferred_element_type=jnp.float32
    )
    row_delta = jnp.einsum("qkgd,qkgd->kgq", grad_rows.astype(jnp.float32), outputs)
    grad_probs = jnp.einsum(
        "qkgd,tkd->kgqt", grad_rows, value_flat, preferred_element_type=jnp.float32
    )
    grad_scores = (score_scale * probabilities * (grad_probs - row_delta[..., None])).astype(
        jnp.bfloat16
    )
    grad_query = jnp.einsum(
        "kgqt,tkd->qkgd", grad_scores, key_flat, preferred_element_type=jnp.float32
    )
    grad_key = jnp.einsum(
        "kgqt,qkgd->tkd", grad_scores, query_rows, preferred_element_type=jnp.float32
    )
    grad_value = jnp.einsum(
        "kgqt,qkgd->tkd", probs_low, grad_rows, preferred_element_type=jnp.float32
    )
    return (
        grad_query.astype(jnp.bfloat16),
        grad_key.reshape(blocks, length, kv_count, head_dim),
        grad_value.reshape(blocks, length, kv_count, head_dim),
    )


def general_body(queries, keys, values, output_gradient, tiles, kinds):
    query_heads, grad_heads, key_heads, value_heads = (
        lax.all_to_all(queries, "space", split_axis=1, concat_axis=0, tiled=True),
        lax.all_to_all(output_gradient, "space", split_axis=1, concat_axis=0, tiled=True),
        lax.all_to_all(keys, "space", split_axis=1, concat_axis=0, tiled=True),
        lax.all_to_all(values, "space", split_axis=1, concat_axis=0, tiled=True),
    )
    window = query_heads.shape[0]
    kv_heads = key_heads.shape[1] // HEAD_SIZE
    head_groups = query_heads.shape[1] // key_heads.shape[1]
    per_window = window // BLOCK_TOKENS
    earlier = [shifted_2((key_heads, value_heads), "tm", offset) for offset in range(1, REACH + 1)]
    tile_count = (REACH + 1) * per_window
    key_tiles = jnp.concatenate([key_heads] + [shifted[0] for shifted in earlier], axis=0)
    key_tiles = key_tiles.reshape(tile_count, BLOCK_TOKENS, kv_heads, HEAD_SIZE)
    value_tiles = jnp.concatenate([value_heads] + [shifted[1] for shifted in earlier], axis=0)
    value_tiles = value_tiles.reshape(tile_count, BLOCK_TOKENS, kv_heads, HEAD_SIZE)
    group_size = math.gcd(per_window, 4)
    rounds = per_window // group_size
    query_groups = query_heads.reshape(
        rounds, group_size, BLOCK_TOKENS, kv_heads, head_groups, HEAD_SIZE
    )
    grad_groups = grad_heads.reshape(
        rounds, group_size, BLOCK_TOKENS, kv_heads, head_groups, HEAD_SIZE
    )
    tile_groups = tiles.reshape(rounds, group_size, MAXT)
    kind_groups = kinds.reshape(rounds, group_size, MAXT)

    def one_round(totals, inputs):
        summed_key_grad, summed_value_grad = totals
        query_part, grad_part, tile_part, kind_part = inputs
        flat_tiles = tile_part.reshape(group_size * MAXT)
        grad_query, grad_key, grad_value = jax.vmap(block_grads)(
            query_part, grad_part, key_tiles[tile_part], value_tiles[tile_part], kind_part
        )
        summed_key_grad = summed_key_grad.at[flat_tiles].add(
            grad_key.reshape(group_size * MAXT, BLOCK_TOKENS, kv_heads, HEAD_SIZE)
        )
        summed_value_grad = summed_value_grad.at[flat_tiles].add(
            grad_value.reshape(group_size * MAXT, BLOCK_TOKENS, kv_heads, HEAD_SIZE)
        )
        return ((summed_key_grad, summed_value_grad), grad_query)

    blank_total_sum = jnp.zeros((tile_count, BLOCK_TOKENS, kv_heads, HEAD_SIZE), jnp.float32)
    (summed_key_grad, summed_value_grad), grad_queries = lax.scan(
        one_round,
        (blank_total_sum, blank_total_sum),
        (query_groups, grad_groups, tile_groups, kind_groups),
    )
    key_parts = summed_key_grad.reshape(REACH + 1, window, kv_heads * HEAD_SIZE)
    value_parts = summed_value_grad.reshape(REACH + 1, window, kv_heads * HEAD_SIZE)
    moving_sum = (key_parts[REACH], value_parts[REACH])
    for offset in range(REACH - 1, -1, -1):
        arrived = shifted_2((moving_sum[0], moving_sum[1]), "tm", -1)
        moving_sum = (arrived[0] + key_parts[offset], arrived[1] + value_parts[offset])
    key_total, value_total = moving_sum
    grad_query_heads = grad_queries.reshape(window, head_groups * kv_heads * HEAD_SIZE)
    return (
        lax.all_to_all(grad_query_heads, "space", split_axis=0, concat_axis=1, tiled=True),
        lax.all_to_all(
            key_total.astype(jnp.bfloat16), "space", split_axis=0, concat_axis=1, tiled=True
        ),
        lax.all_to_all(
            value_total.astype(jnp.bfloat16), "space", split_axis=0, concat_axis=1, tiled=True
        ),
    )


def packed(arrays, half, first, width):
    start = half * (arrays[0].shape[1] // 2) + first
    return jnp.concatenate([lax.dynamic_slice_in_dim(a, start, width, 1) for a in arrays], axis=0)


def dot(a, b, contract):
    return lax.dot_general(a, b, ((contract[:1], contract[1:]), ((), ())), preferred_element_type=jnp.float32)


def find_limits(side, code_ref, limit_ref):
    for r in range(2):
        block = side if r == 0 else 1 - side
        codes = [code_ref[block * MAXT + m] for m in range(MAXT)]
        for p in range(2 * (REACH + 1)):
            value = p // 2 * 2 + (side if p % 2 == 0 else 1 - side)
            limit = -FAR
            for code in codes:
                limit = jnp.where(code == 4 * value, FAR, jnp.where(code == 4 * value + 1, 0, limit))
            limit_ref[r * 6 + p] = limit


def attend_kernel(
    side_ref, code_ref,
    q_own, g_own, qg_other, k_own, v_own, kv_other, kv2_own, kv2_other, kv1,
    dq_own, dq_other, d0, d1, d2_own, d2_other,
    limit_ref, *scratch,
):
    n, d = BLOCK_TOKENS, HEAD_SIZE

    @pl.when(pl.program_id(0) == 0)
    def _():
        find_limits(side_ref[0], code_ref, limit_ref)

    lanes = 2 * n
    column = lax.broadcasted_iota(jnp.int32, (n, lanes), 0)
    row = lax.broadcasted_iota(jnp.int32, (n, lanes), 1)
    ahead = column - jnp.where(row >= n, row - n, row)
    scale = 1.0 / math.sqrt(d)
    rate = scale * math.log2(math.e)
    for h in range(STEP_HEADS):
        q_all, g_all, k_all, v_all, s_ref, dp_ref, p_ref, ds_ref = scratch[8 * h : 8 * h + 8]
        wide, slim = slice(2 * h * d, 2 * (h + 1) * d), slice(h * d, (h + 1) * d)
        for r, (q, g) in enumerate(
            ((q_own[:, wide], g_own[:, wide]), (qg_other[:n, wide], qg_other[n:, wide]))
        ):
            for j in range(2):
                rows = slice((2 * r + j) * n, (2 * r + j + 1) * n)
                q_all[rows, :] = q[:, j * d : (j + 1) * d]
                g_all[rows, :] = g[:, j * d : (j + 1) * d]
        tiles = (
            (k_own[:, slim], v_own[:, slim]),
            (kv_other[:n, slim], kv_other[n:, slim]),
            (kv1[:n, slim], kv1[n : 2 * n, slim]),
            (kv1[2 * n : 3 * n, slim], kv1[3 * n :, slim]),
            (kv2_own[:n, slim], kv2_own[n:, slim]),
            (kv2_other[:n, slim], kv2_other[n:, slim]),
        )
        for p, (k, v) in enumerate(tiles):
            k_all[p * n : (p + 1) * n, :] = k
            v_all[p * n : (p + 1) * n, :] = v
        for r in range(2):
            cols = slice(r * lanes, (r + 1) * lanes)
            q, g = q_all[cols, :], g_all[cols, :]
            top = None
            for p in range(6):
                rows = slice(p * n, (p + 1) * n)
                s = dot(k_all[rows, :], q, (1, 1))
                s = jnp.where(ahead <= limit_ref[r * 6 + p], s, HIDDEN)
                s_ref[rows, :] = s
                high = jnp.max(s, axis=0, keepdims=True)
                top = high if top is None else jnp.maximum(top, high)
            total = jnp.zeros((1, lanes), jnp.float32)
            delta = jnp.zeros((1, lanes), jnp.float32)
            for p in range(6):
                rows = slice(p * n, (p + 1) * n)
                e = jnp.exp2((s_ref[rows, :] - top) * rate)
                dp = dot(v_all[rows, :], g, (1, 1))
                s_ref[rows, :] = e
                dp_ref[rows, :] = dp
                total = total + jnp.sum(e, axis=0, keepdims=True)
                delta = delta + jnp.sum(e * dp, axis=0, keepdims=True)
            share = 1.0 / total
            delta = delta * share
            for p in range(6):
                rows = slice(p * n, (p + 1) * n)
                prob = s_ref[rows, :] * share
                ds = prob * (dp_ref[rows, :] - delta)
                p_ref[rows, cols] = prob.astype(jnp.bfloat16)
                ds_ref[rows, cols] = ds.astype(jnp.bfloat16)
        dk = dot(ds_ref[...], q_all[...], (1, 0)) * scale
        dv = dot(p_ref[...], g_all[...], (1, 0))
        homes = ((d0, 0), (d0, 2), (d1, 0), (d1, 2), (d2_own, 0), (d2_other, 0))
        for p, (out, place) in enumerate(homes):
            rows = slice(p * n, (p + 1) * n)
            out[place * n : (place + 1) * n, slim] = dk[rows].astype(out.dtype)
            out[(place + 1) * n : (place + 2) * n, slim] = dv[rows].astype(out.dtype)
        dq = (dot(k_all[...], ds_ref[...], (0, 0)) * scale).T.astype(jnp.bfloat16)
        for j in range(2):
            here = slice((2 * h + j) * d, (2 * h + j + 1) * d)
            dq_own[:, here] = dq[j * n : (j + 1) * n, :]
            dq_other[:, here] = dq[(2 + j) * n : (3 + j) * n, :]


def attend(side, limits, first, heads, queries, grads, keys, values, qg_other, kv_other, kv2_own, kv2_other, kv1):
    n, d = BLOCK_TOKENS, HEAD_SIZE
    steps = heads // STEP_HEADS
    per_side = keys.shape[1] // (2 * d * STEP_HEADS)
    slim, wide = STEP_HEADS * d, 2 * STEP_HEADS * d

    def mine(h, side_ref, code_ref):
        return 0, side_ref[0] * per_side + first // STEP_HEADS + h

    def here(h, side_ref, code_ref):
        return 0, h

    def out(rows, width, dtype):
        return (
            jax.ShapeDtypeStruct((rows, steps * width), dtype),
            pl.BlockSpec((rows, width), here),
        )

    outs = [
        out(n, wide, jnp.bfloat16),
        out(n, wide, jnp.bfloat16),
        out(4 * n, slim, jnp.float32),
        out(4 * n, slim, jnp.bfloat16),
        out(2 * n, slim, jnp.bfloat16),
        out(2 * n, slim, jnp.bfloat16),
    ]
    work = [
        pltpu.VMEM((4 * n, d), jnp.bfloat16),
        pltpu.VMEM((4 * n, d), jnp.bfloat16),
        pltpu.VMEM((6 * n, d), jnp.bfloat16),
        pltpu.VMEM((6 * n, d), jnp.bfloat16),
        pltpu.VMEM((6 * n, 2 * n), jnp.float32),
        pltpu.VMEM((6 * n, 2 * n), jnp.float32),
        pltpu.VMEM((6 * n, 4 * n), jnp.bfloat16),
        pltpu.VMEM((6 * n, 4 * n), jnp.bfloat16),
    ]
    return pl.pallas_call(
        attend_kernel,
        grid_spec=pltpu.PrefetchScalarGridSpec(
            num_scalar_prefetch=2,
            grid=(steps,),
            in_specs=[
                pl.BlockSpec((n, wide), mine),
                pl.BlockSpec((n, wide), mine),
                pl.BlockSpec((2 * n, wide), here),
                pl.BlockSpec((n, slim), mine),
                pl.BlockSpec((n, slim), mine),
                pl.BlockSpec((2 * n, slim), here),
                pl.BlockSpec((2 * n, slim), here),
                pl.BlockSpec((2 * n, slim), here),
                pl.BlockSpec((4 * n, slim), here),
            ],
            out_specs=[spec for _, spec in outs],
            scratch_shapes=[pltpu.SMEM((12,), jnp.int32)] + work * STEP_HEADS,
        ),
        out_shape=[shape for shape, _ in outs],
        compiler_params=pltpu.CompilerParams(vmem_limit_bytes=VMEM_BYTES),
    )(side, limits, queries, grads, qg_other, keys, values, kv_other, kv2_own, kv2_other, kv1)


def swap(block):
    return lax.ppermute(block, "space", [(0, 1), (1, 0)])


def mate(block):
    return lax.ppermute(block, "tm", [(i, i ^ 1) for i in range(lax.axis_size("tm"))])


def moved(block, distance):
    size = lax.axis_size("tm")
    return lax.ppermute(
        block, "tm", [(i, i + distance) for i in range(size) if 0 <= i + distance < size]
    )


def after(arrays, *earlier):
    arrays = list(arrays)
    return lax.optimization_barrier((*arrays, *earlier))[: len(arrays)]


def pair_body(queries, keys, values, output_gradient, tiles, kinds):
    n, d = BLOCK_TOKENS, HEAD_SIZE
    side = lax.axis_index("space")
    odd = lax.axis_index("tm") % 2 == 1
    half = keys.shape[1] // (2 * d)
    sizes = [half // 2, half - half // 2]
    firsts = [0, half // 2]
    place = side.reshape(1).astype(jnp.int32)
    codes = 4 * tiles + kinds
    limits = jnp.concatenate([codes[0], codes[1]])

    def kv_part(part, c, *earlier):
        return packed(after([keys, values], *earlier), part, firsts[c] * d, sizes[c] * d)

    def qg_part(part, c, *earlier):
        arrays = after([queries, output_gradient], *earlier)
        return packed(arrays, part, 2 * firsts[c] * d, 2 * sizes[c] * d)

    kv_away = [kv_part(1 - side, 0)]
    kv_away.append(kv_part(1 - side, 1, kv_away[0]))
    kv_own = [kv_part(side, 0, kv_away[1])]
    qg_away = [qg_part(1 - side, 0, kv_own[0])]
    qg_away.append(qg_part(1 - side, 1, qg_away[0]))
    kv_own.append(kv_part(side, 1, qg_away[1]))

    kv_other = [swap(b) for b in kv_away]
    qg_other = [swap(b) for b in qg_away]
    kv2_own = [moved(b, 2) for b in kv_own]
    kv2_other = [moved(b, 2) for b in kv_other]

    def attended(c, *earlier):
        kv1 = mate(
            jnp.concatenate(
                [
                    jnp.where(odd, kv2_own[c], kv_own[c]),
                    jnp.where(odd, kv2_other[c], kv_other[c]),
                ],
                axis=0,
            )
        )
        return attend(
            place, after([limits], *earlier)[0] if earlier else limits, firsts[c], sizes[c],
            queries, output_gradient, keys, values,
            qg_other[c], kv_other[c], kv2_own[c], kv2_other[c], kv1,
        )

    def met(d1):
        both = mate(d1).astype(jnp.float32)
        return jnp.where(odd, both, 0.0), jnp.where(odd, 0.0, both)

    def low(total):
        return total.astype(jnp.bfloat16)

    dq_own0, dq_away0, e0, d1, d2_own, d2_other = attended(0)
    dq_other0 = swap(dq_away0)
    met_back, met_here0 = met(d1)
    ship0 = low(jnp.concatenate([d2_own, d2_other], axis=0) + met_back)
    back0 = moved(ship0, -2)
    dq_own1, dq_away1, d0, d1, d2_own, d2_other = attended(1, ship0)
    d1, dq_other0 = after([d1, dq_other0])
    dq_other1 = swap(dq_away1)
    met_back, met_here = met(d1)
    ship_other = low(d2_other + met_back[2 * n :])
    ship_own = low(d2_own + met_back[: 2 * n])
    back_other = moved(ship_other, -2)
    back_own = moved(ship_own, -2)
    sum0 = low(e0 + met_here0 + back0)
    own0 = sum0[: 2 * n]
    other0 = swap(sum0[2 * n :])
    sum_other = low(d0[2 * n :] + met_here[2 * n :] + back_other)
    other1 = swap(sum_other)
    own1 = low(d0[: 2 * n] + met_here[: 2 * n] + back_own)

    def placed(own, other):
        own, other = jnp.concatenate(own, axis=1), jnp.concatenate(other, axis=1)
        return jnp.where(
            side == 0,
            jnp.concatenate([own, other], axis=1),
            jnp.concatenate([other, own], axis=1),
        )

    dq_own0, dq_own1, dq_other0, dq_other1 = after(
        [dq_own0, dq_own1, dq_other0, dq_other1], ship_other, ship_own
    )
    grad_queries = placed([dq_own0, dq_own1], [dq_other0, dq_other1])
    return (
        grad_queries,
        placed([own0[:n], own1[:n]], [other0[:n], other1[:n]]),
        placed([own0[n:], own1[n:]], [other0[n:], other1[n:]]),
    )


def body(queries, keys, values, output_gradient, tiles, kinds):
    pair = (
        lax.axis_size("space") == 2
        and lax.axis_size("tm") % 2 == 0
        and tiles.shape[0] == 2
        and queries.shape[0] == BLOCK_TOKENS
        and queries.shape[1] == 2 * keys.shape[1]
        and keys.shape[1] % (4 * HEAD_SIZE) == 0
    )
    run = pair_body if pair else general_body
    return run(queries, keys, values, output_gradient, tiles, kinds)


def solution(mesh):
    in_specs = (
        P(("tm", "space"), None),
        P(("tm", "space"), None),
        P(("tm", "space"), None),
        P(("tm", "space"), None),
        P("tm", None),
        P("tm", None),
    )
    out_specs = (P(("tm", "space"), None), P(("tm", "space"), None), P(("tm", "space"), None))
    return jax.shard_map(body, mesh=mesh, in_specs=in_specs, out_specs=out_specs, check_vma=False)
```

```python
import math

import jax
import jax.numpy as jnp
from jax import lax
from jax.experimental import pallas as pl
from jax.experimental.pallas import tpu as pltpu
from jax.sharding import PartitionSpec as P

HEAD_SIZE = 128
BLOCK_TOKENS = 128
MAXT = 6
REACH = 2
STEP_HEADS = 1
HIDDEN = -1e30
FAR = 1 << 20
VMEM_BYTES = 57344 * 1024


def shifted_2(block, axis, distance):
    devices = range(lax.axis_size(axis))
    route = [(i - distance, i) for i in devices if i - distance in devices]
    return lax.ppermute(block, axis, route)


def block_grads(query_rows, grad_rows, key_tiles, value_tiles, tile_kinds):
    blocks, length, kv_count, head_dim = key_tiles.shape
    score_scale = 1.0 / head_dim**0.5
    key_flat = key_tiles.reshape(blocks * length, kv_count, head_dim)
    value_flat = value_tiles.reshape(blocks * length, kv_count, head_dim)
    scores = (
        jnp.einsum("qkgd,tkd->kgqt", query_rows, key_flat, preferred_element_type=jnp.float32)
        * score_scale
    )
    query_pos = jnp.arange(length)
    column_kind = jnp.repeat(tile_kinds, length)
    column_pos = jnp.tile(jnp.arange(length), blocks)
    visible = (column_kind == 0)[None, :] | (column_kind == 1)[None, :] & (
        column_pos[None, :] <= query_pos[:, None]
    )
    masked = jnp.where(visible, scores, -jnp.inf)
    row_max = jnp.max(masked, axis=-1, keepdims=True)
    weights = jnp.where(visible, jnp.exp(masked - row_max), 0.0)
    probabilities = weights / jnp.sum(weights, axis=-1, keepdims=True)
    probs_low = probabilities.astype(jnp.bfloat16)
    outputs = jnp.einsum(
        "kgqt,tkd->qkgd", probs_low, value_flat, preferred_element_type=jnp.float32
    )
    row_delta = jnp.einsum("qkgd,qkgd->kgq", grad_rows.astype(jnp.float32), outputs)
    grad_probs = jnp.einsum(
        "qkgd,tkd->kgqt", grad_rows, value_flat, preferred_element_type=jnp.float32
    )
    grad_scores = (score_scale * probabilities * (grad_probs - row_delta[..., None])).astype(
        jnp.bfloat16
    )
    grad_query = jnp.einsum(
        "kgqt,tkd->qkgd", grad_scores, key_flat, preferred_element_type=jnp.float32
    )
    grad_key = jnp.einsum(
        "kgqt,qkgd->tkd", grad_scores, query_rows, preferred_element_type=jnp.float32
    )
    grad_value = jnp.einsum(
        "kgqt,qkgd->tkd", probs_low, grad_rows, preferred_element_type=jnp.float32
    )
    return (
        grad_query.astype(jnp.bfloat16),
        grad_key.reshape(blocks, length, kv_count, head_dim),
        grad_value.reshape(blocks, length, kv_count, head_dim),
    )


def general_body(queries, keys, values, output_gradient, tiles, kinds):
    query_heads, grad_heads, key_heads, value_heads = (
        lax.all_to_all(queries, "space", split_axis=1, concat_axis=0, tiled=True),
        lax.all_to_all(output_gradient, "space", split_axis=1, concat_axis=0, tiled=True),
        lax.all_to_all(keys, "space", split_axis=1, concat_axis=0, tiled=True),
        lax.all_to_all(values, "space", split_axis=1, concat_axis=0, tiled=True),
    )
    window = query_heads.shape[0]
    kv_heads = key_heads.shape[1] // HEAD_SIZE
    head_groups = query_heads.shape[1] // key_heads.shape[1]
    per_window = window // BLOCK_TOKENS
    earlier = [shifted_2((key_heads, value_heads), "tm", offset) for offset in range(1, REACH + 1)]
    tile_count = (REACH + 1) * per_window
    key_tiles = jnp.concatenate([key_heads] + [shifted[0] for shifted in earlier], axis=0)
    key_tiles = key_tiles.reshape(tile_count, BLOCK_TOKENS, kv_heads, HEAD_SIZE)
    value_tiles = jnp.concatenate([value_heads] + [shifted[1] for shifted in earlier], axis=0)
    value_tiles = value_tiles.reshape(tile_count, BLOCK_TOKENS, kv_heads, HEAD_SIZE)
    group_size = math.gcd(per_window, 4)
    rounds = per_window // group_size
    query_groups = query_heads.reshape(
        rounds, group_size, BLOCK_TOKENS, kv_heads, head_groups, HEAD_SIZE
    )
    grad_groups = grad_heads.reshape(
        rounds, group_size, BLOCK_TOKENS, kv_heads, head_groups, HEAD_SIZE
    )
    tile_groups = tiles.reshape(rounds, group_size, MAXT)
    kind_groups = kinds.reshape(rounds, group_size, MAXT)

    def one_round(totals, inputs):
        summed_key_grad, summed_value_grad = totals
        query_part, grad_part, tile_part, kind_part = inputs
        flat_tiles = tile_part.reshape(group_size * MAXT)
        grad_query, grad_key, grad_value = jax.vmap(block_grads)(
            query_part, grad_part, key_tiles[tile_part], value_tiles[tile_part], kind_part
        )
        summed_key_grad = summed_key_grad.at[flat_tiles].add(
            grad_key.reshape(group_size * MAXT, BLOCK_TOKENS, kv_heads, HEAD_SIZE)
        )
        summed_value_grad = summed_value_grad.at[flat_tiles].add(
            grad_value.reshape(group_size * MAXT, BLOCK_TOKENS, kv_heads, HEAD_SIZE)
        )
        return ((summed_key_grad, summed_value_grad), grad_query)

    blank_total_sum = jnp.zeros((tile_count, BLOCK_TOKENS, kv_heads, HEAD_SIZE), jnp.float32)
    (summed_key_grad, summed_value_grad), grad_queries = lax.scan(
        one_round,
        (blank_total_sum, blank_total_sum),
        (query_groups, grad_groups, tile_groups, kind_groups),
    )
    key_parts = summed_key_grad.reshape(REACH + 1, window, kv_heads * HEAD_SIZE)
    value_parts = summed_value_grad.reshape(REACH + 1, window, kv_heads * HEAD_SIZE)
    moving_sum = (key_parts[REACH], value_parts[REACH])
    for offset in range(REACH - 1, -1, -1):
        arrived = shifted_2((moving_sum[0], moving_sum[1]), "tm", -1)
        moving_sum = (arrived[0] + key_parts[offset], arrived[1] + value_parts[offset])
    key_total, value_total = moving_sum
    grad_query_heads = grad_queries.reshape(window, head_groups * kv_heads * HEAD_SIZE)
    return (
        lax.all_to_all(grad_query_heads, "space", split_axis=0, concat_axis=1, tiled=True),
        lax.all_to_all(
            key_total.astype(jnp.bfloat16), "space", split_axis=0, concat_axis=1, tiled=True
        ),
        lax.all_to_all(
            value_total.astype(jnp.bfloat16), "space", split_axis=0, concat_axis=1, tiled=True
        ),
    )


def packed(arrays, half, first, width):
    start = half * (arrays[0].shape[1] // 2) + first
    return jnp.concatenate([lax.dynamic_slice_in_dim(a, start, width, 1) for a in arrays], axis=0)


def dot(a, b, contract):
    return lax.dot_general(a, b, ((contract[:1], contract[1:]), ((), ())), preferred_element_type=jnp.float32)


def find_limits(side, code_ref, limit_ref):
    for r in range(2):
        block = side if r == 0 else 1 - side
        codes = [code_ref[block * MAXT + m] for m in range(MAXT)]
        for p in range(2 * (REACH + 1)):
            value = p // 2 * 2 + (side if p % 2 == 0 else 1 - side)
            limit = -FAR
            for code in codes:
                limit = jnp.where(code == 4 * value, FAR, jnp.where(code == 4 * value + 1, 0, limit))
            limit_ref[r * 6 + p] = limit


def attend_kernel(
    side_ref, code_ref,
    q_own, g_own, qg_other, k_own, v_own, kv_other, kv2_own, kv2_other, kv1,
    dq_own, dq_other, d0_own, d0_other, d1_own, d1_other, d2_own, d2_other,
    limit_ref, *scratch,
):
    n, d = BLOCK_TOKENS, HEAD_SIZE

    @pl.when(pl.program_id(0) == 0)
    def _():
        find_limits(side_ref[0], code_ref, limit_ref)

    lanes = 2 * n
    column = lax.broadcasted_iota(jnp.int32, (n, lanes), 0)
    row = lax.broadcasted_iota(jnp.int32, (n, lanes), 1)
    ahead = column - jnp.where(row >= n, row - n, row)
    scale = 1.0 / math.sqrt(d)
    rate = scale * math.log2(math.e)
    for h in range(STEP_HEADS):
        q_all, g_all, k_all, v_all, s_ref, dp_ref, p_ref, ds_ref = scratch[8 * h : 8 * h + 8]
        wide, slim = slice(2 * h * d, 2 * (h + 1) * d), slice(h * d, (h + 1) * d)
        for r, (q, g) in enumerate(
            ((q_own[:, wide], g_own[:, wide]), (qg_other[:n, wide], qg_other[n:, wide]))
        ):
            for j in range(2):
                rows = slice((2 * r + j) * n, (2 * r + j + 1) * n)
                q_all[rows, :] = q[:, j * d : (j + 1) * d]
                g_all[rows, :] = g[:, j * d : (j + 1) * d]
        tiles = (
            (k_own[:, slim], v_own[:, slim]),
            (kv_other[:n, slim], kv_other[n:, slim]),
            (kv1[:n, slim], kv1[n : 2 * n, slim]),
            (kv1[2 * n : 3 * n, slim], kv1[3 * n :, slim]),
            (kv2_own[:n, slim], kv2_own[n:, slim]),
            (kv2_other[:n, slim], kv2_other[n:, slim]),
        )
        for p, (k, v) in enumerate(tiles):
            k_all[p * n : (p + 1) * n, :] = k
            v_all[p * n : (p + 1) * n, :] = v
        for r in range(2):
            cols = slice(r * lanes, (r + 1) * lanes)
            q, g = q_all[cols, :], g_all[cols, :]
            top = None
            for p in range(6):
                rows = slice(p * n, (p + 1) * n)
                s = dot(k_all[rows, :], q, (1, 1))
                s = jnp.where(ahead <= limit_ref[r * 6 + p], s, HIDDEN)
                s_ref[rows, :] = s
                high = jnp.max(s.reshape(n // 8, 8, lanes), axis=0)
                top = high if top is None else jnp.maximum(top, high)
            top = jnp.max(top, axis=0, keepdims=True)
            total = jnp.zeros((8, lanes), jnp.float32)
            delta = jnp.zeros((8, lanes), jnp.float32)
            for p in range(6):
                rows = slice(p * n, (p + 1) * n)
                e = jnp.exp2((s_ref[rows, :] - top) * rate)
                dp = dot(v_all[rows, :], g, (1, 1))
                s_ref[rows, :] = e
                dp_ref[rows, :] = dp
                total = total + jnp.sum(e.reshape(n // 8, 8, lanes), axis=0)
                delta = delta + jnp.sum((e * dp).reshape(n // 8, 8, lanes), axis=0)
            share = 1.0 / jnp.sum(total, axis=0, keepdims=True)
            delta = jnp.sum(delta, axis=0, keepdims=True) * share
            for p in range(6):
                rows = slice(p * n, (p + 1) * n)
                prob = s_ref[rows, :] * share
                ds = prob * (dp_ref[rows, :] - delta)
                p_ref[rows, cols] = prob.astype(jnp.bfloat16)
                ds_ref[rows, cols] = ds.astype(jnp.bfloat16)
        dk = dot(ds_ref[...], q_all[...], (1, 0)) * scale
        dv = dot(p_ref[...], g_all[...], (1, 0))
        for p, out in enumerate((d0_own, d0_other, d1_own, d1_other, d2_own, d2_other)):
            rows = slice(p * n, (p + 1) * n)
            out[:n, slim] = dk[rows].astype(out.dtype)
            out[n:, slim] = dv[rows].astype(out.dtype)
        dq = (dot(k_all[...], ds_ref[...], (0, 0)) * scale).T.astype(jnp.bfloat16)
        for j in range(2):
            here = slice((2 * h + j) * d, (2 * h + j + 1) * d)
            dq_own[:, here] = dq[j * n : (j + 1) * n, :]
            dq_other[:, here] = dq[(2 + j) * n : (3 + j) * n, :]


def attend(side, limits, first, heads, queries, grads, keys, values, qg_other, kv_other, kv2_own, kv2_other, kv1):
    n, d = BLOCK_TOKENS, HEAD_SIZE
    steps = heads // STEP_HEADS
    per_side = keys.shape[1] // (2 * d * STEP_HEADS)
    slim, wide = STEP_HEADS * d, 2 * STEP_HEADS * d

    def mine(h, side_ref, code_ref):
        return 0, side_ref[0] * per_side + first // STEP_HEADS + h

    def here(h, side_ref, code_ref):
        return 0, h

    def out(rows, width, dtype):
        return (
            jax.ShapeDtypeStruct((rows, steps * width), dtype),
            pl.BlockSpec((rows, width), here),
        )

    outs = [
        out(n, wide, jnp.bfloat16),
        out(n, wide, jnp.bfloat16),
        out(2 * n, slim, jnp.float32),
        out(2 * n, slim, jnp.float32),
        out(2 * n, slim, jnp.bfloat16),
        out(2 * n, slim, jnp.bfloat16),
        out(2 * n, slim, jnp.bfloat16),
        out(2 * n, slim, jnp.bfloat16),
    ]
    work = [
        pltpu.VMEM((4 * n, d), jnp.bfloat16),
        pltpu.VMEM((4 * n, d), jnp.bfloat16),
        pltpu.VMEM((6 * n, d), jnp.bfloat16),
        pltpu.VMEM((6 * n, d), jnp.bfloat16),
        pltpu.VMEM((6 * n, 2 * n), jnp.float32),
        pltpu.VMEM((6 * n, 2 * n), jnp.float32),
        pltpu.VMEM((6 * n, 4 * n), jnp.bfloat16),
        pltpu.VMEM((6 * n, 4 * n), jnp.bfloat16),
    ]
    return pl.pallas_call(
        attend_kernel,
        grid_spec=pltpu.PrefetchScalarGridSpec(
            num_scalar_prefetch=2,
            grid=(steps,),
            in_specs=[
                pl.BlockSpec((n, wide), mine),
                pl.BlockSpec((n, wide), mine),
                pl.BlockSpec((2 * n, wide), here),
                pl.BlockSpec((n, slim), mine),
                pl.BlockSpec((n, slim), mine),
                pl.BlockSpec((2 * n, slim), here),
                pl.BlockSpec((2 * n, slim), here),
                pl.BlockSpec((2 * n, slim), here),
                pl.BlockSpec((4 * n, slim), here),
            ],
            out_specs=[spec for _, spec in outs],
            scratch_shapes=[pltpu.SMEM((12,), jnp.int32)] + work * STEP_HEADS,
        ),
        out_shape=[shape for shape, _ in outs],
        compiler_params=pltpu.CompilerParams(vmem_limit_bytes=VMEM_BYTES),
    )(side, limits, queries, grads, qg_other, keys, values, kv_other, kv2_own, kv2_other, kv1)


def swap(block):
    return lax.ppermute(block, "space", [(0, 1), (1, 0)])


def mate(block):
    return lax.ppermute(block, "tm", [(i, i ^ 1) for i in range(lax.axis_size("tm"))])


def moved(block, distance):
    size = lax.axis_size("tm")
    return lax.ppermute(
        block, "tm", [(i, i + distance) for i in range(size) if 0 <= i + distance < size]
    )


def after(arrays, *earlier):
    arrays = list(arrays)
    return lax.optimization_barrier((*arrays, *earlier))[: len(arrays)]


def pair_body(queries, keys, values, output_gradient, tiles, kinds):
    n, d = BLOCK_TOKENS, HEAD_SIZE
    side = lax.axis_index("space")
    odd = lax.axis_index("tm") % 2 == 1
    half = keys.shape[1] // (2 * d)
    sizes = [half // 2, half - half // 2]
    firsts = [0, half // 2]
    place = side.reshape(1).astype(jnp.int32)
    codes = 4 * tiles + kinds
    limits = jnp.concatenate([codes[0], codes[1]])

    def kv_part(part, c, *earlier):
        return packed(after([keys, values], *earlier), part, firsts[c] * d, sizes[c] * d)

    def qg_part(part, c, *earlier):
        arrays = after([queries, output_gradient], *earlier)
        return packed(arrays, part, 2 * firsts[c] * d, 2 * sizes[c] * d)

    kv_away = [kv_part(1 - side, 0)]
    kv_away.append(kv_part(1 - side, 1, kv_away[0]))
    kv_own = [kv_part(side, 0, kv_away[1])]
    qg_away = [qg_part(1 - side, 0, kv_own[0])]
    qg_away.append(qg_part(1 - side, 1, qg_away[0]))
    kv_own.append(kv_part(side, 1, qg_away[1]))

    kv_other = [swap(b) for b in kv_away]
    qg_other = [swap(b) for b in qg_away]
    kv2_own, kv2_other = [moved(kv_own[0], 2)], [moved(kv_other[0], 2)]
    late = moved(jnp.concatenate([kv_own[1], kv_other[1]], axis=0), 2)
    kv2_own.append(late[: 2 * n])
    kv2_other.append(late[2 * n :])

    def attended(c, *earlier):
        kv1 = mate(
            jnp.concatenate(
                [
                    jnp.where(odd, kv2_own[c], kv_own[c]),
                    jnp.where(odd, kv2_other[c], kv_other[c]),
                ],
                axis=0,
            )
        )
        return attend(
            place, after([limits], *earlier)[0] if earlier else limits, firsts[c], sizes[c],
            queries, output_gradient, keys, values,
            qg_other[c], kv_other[c], kv2_own[c], kv2_other[c], kv1,
        )

    def low(total):
        return total.astype(jnp.bfloat16)

    def back_sum(own, met):
        return low(own + jnp.where(odd, met.astype(jnp.float32), 0.0))

    def here_sum(own, met, back):
        return low(own + jnp.where(odd, 0.0, met.astype(jnp.float32)) + back)

    dq_own0, dq_away0, e0_own, e0_other, e1_own, e1_other, e2_own, e2_other = attended(0)
    e1_own, e1_other = after([e1_own, e1_other], qg_other[1])
    dq_other0 = swap(dq_away0)
    e1_own, e1_other = mate(e1_own), mate(e1_other)
    ship0 = [jnp.concatenate([back_sum(e2_own, e1_own), back_sum(e2_other, e1_other)], axis=0)]
    back0 = moved(ship0[0], -2)
    back_own0, back_other0 = back0[: 2 * n], back0[2 * n :]

    dq_own1, dq_away1, d0_own, d0_other, d1_own, d1_other, d2_own, d2_other = attended(1, *ship0)
    d1_own, d1_other, back_other0 = after([d1_own, d1_other, back_other0])
    dq_other1 = swap(dq_away1)
    d1_other = mate(d1_other)
    d1_own = mate(d1_own)
    ship_other = back_sum(d2_other, d1_other)
    back_other = moved(ship_other, -2)
    ship_own = back_sum(d2_own, d1_own)
    back_own = moved(ship_own, -2)
    other0 = swap(here_sum(e0_other, e1_other, back_other0))
    other1 = swap(here_sum(d0_other, d1_other, back_other))
    own0 = here_sum(e0_own, e1_own, back_own0)
    own1 = here_sum(d0_own, d1_own, back_own)

    def placed(own, other):
        own, other = jnp.concatenate(own, axis=1), jnp.concatenate(other, axis=1)
        return jnp.where(
            side == 0,
            jnp.concatenate([own, other], axis=1),
            jnp.concatenate([other, own], axis=1),
        )

    dq_own0, dq_own1, dq_other0, dq_other1 = after(
        [dq_own0, dq_own1, dq_other0, dq_other1], ship_other, ship_own
    )
    grad_queries = placed([dq_own0, dq_own1], [dq_other0, dq_other1])
    return (
        grad_queries,
        placed([own0[:n], own1[:n]], [other0[:n], other1[:n]]),
        placed([own0[n:], own1[n:]], [other0[n:], other1[n:]]),
    )


def body(queries, keys, values, output_gradient, tiles, kinds):
    pair = (
        lax.axis_size("space") == 2
        and lax.axis_size("tm") % 2 == 0
        and tiles.shape[0] == 2
        and queries.shape[0] == BLOCK_TOKENS
        and queries.shape[1] == 2 * keys.shape[1]
        and keys.shape[1] % (4 * HEAD_SIZE) == 0
    )
    run = pair_body if pair else general_body
    return run(queries, keys, values, output_gradient, tiles, kinds)


def solution(mesh):
    in_specs = (
        P(("tm", "space"), None),
        P(("tm", "space"), None),
        P(("tm", "space"), None),
        P(("tm", "space"), None),
        P("tm", None),
        P("tm", None),
    )
    out_specs = (P(("tm", "space"), None), P(("tm", "space"), None), P(("tm", "space"), None))
    return jax.shard_map(body, mesh=mesh, in_specs=in_specs, out_specs=out_specs, check_vma=False)
```

```python
import math

import jax
import jax.numpy as jnp
from jax import lax
from jax.experimental import pallas as pl
from jax.experimental.pallas import tpu as pltpu
from jax.sharding import PartitionSpec as P

HEAD_SIZE = 128
BLOCK_TOKENS = 128
MAXT = 6
REACH = 2
STEP_HEADS = 1
HIDDEN = -1e30
FAR = 1 << 20
VMEM_BYTES = 57344 * 1024


def shifted_2(block, axis, distance):
    devices = range(lax.axis_size(axis))
    route = [(i - distance, i) for i in devices if i - distance in devices]
    return lax.ppermute(block, axis, route)


def block_grads(query_rows, grad_rows, key_tiles, value_tiles, tile_kinds):
    blocks, length, kv_count, head_dim = key_tiles.shape
    score_scale = 1.0 / head_dim**0.5
    key_flat = key_tiles.reshape(blocks * length, kv_count, head_dim)
    value_flat = value_tiles.reshape(blocks * length, kv_count, head_dim)
    scores = (
        jnp.einsum("qkgd,tkd->kgqt", query_rows, key_flat, preferred_element_type=jnp.float32)
        * score_scale
    )
    query_pos = jnp.arange(length)
    column_kind = jnp.repeat(tile_kinds, length)
    column_pos = jnp.tile(jnp.arange(length), blocks)
    visible = (column_kind == 0)[None, :] | (column_kind == 1)[None, :] & (
        column_pos[None, :] <= query_pos[:, None]
    )
    masked = jnp.where(visible, scores, -jnp.inf)
    row_max = jnp.max(masked, axis=-1, keepdims=True)
    weights = jnp.where(visible, jnp.exp(masked - row_max), 0.0)
    probabilities = weights / jnp.sum(weights, axis=-1, keepdims=True)
    probs_low = probabilities.astype(jnp.bfloat16)
    outputs = jnp.einsum(
        "kgqt,tkd->qkgd", probs_low, value_flat, preferred_element_type=jnp.float32
    )
    row_delta = jnp.einsum("qkgd,qkgd->kgq", grad_rows.astype(jnp.float32), outputs)
    grad_probs = jnp.einsum(
        "qkgd,tkd->kgqt", grad_rows, value_flat, preferred_element_type=jnp.float32
    )
    grad_scores = (score_scale * probabilities * (grad_probs - row_delta[..., None])).astype(
        jnp.bfloat16
    )
    grad_query = jnp.einsum(
        "kgqt,tkd->qkgd", grad_scores, key_flat, preferred_element_type=jnp.float32
    )
    grad_key = jnp.einsum(
        "kgqt,qkgd->tkd", grad_scores, query_rows, preferred_element_type=jnp.float32
    )
    grad_value = jnp.einsum(
        "kgqt,qkgd->tkd", probs_low, grad_rows, preferred_element_type=jnp.float32
    )
    return (
        grad_query.astype(jnp.bfloat16),
        grad_key.reshape(blocks, length, kv_count, head_dim),
        grad_value.reshape(blocks, length, kv_count, head_dim),
    )


def general_body(queries, keys, values, output_gradient, tiles, kinds):
    query_heads, grad_heads, key_heads, value_heads = (
        lax.all_to_all(queries, "space", split_axis=1, concat_axis=0, tiled=True),
        lax.all_to_all(output_gradient, "space", split_axis=1, concat_axis=0, tiled=True),
        lax.all_to_all(keys, "space", split_axis=1, concat_axis=0, tiled=True),
        lax.all_to_all(values, "space", split_axis=1, concat_axis=0, tiled=True),
    )
    window = query_heads.shape[0]
    kv_heads = key_heads.shape[1] // HEAD_SIZE
    head_groups = query_heads.shape[1] // key_heads.shape[1]
    per_window = window // BLOCK_TOKENS
    earlier = [shifted_2((key_heads, value_heads), "tm", offset) for offset in range(1, REACH + 1)]
    tile_count = (REACH + 1) * per_window
    key_tiles = jnp.concatenate([key_heads] + [shifted[0] for shifted in earlier], axis=0)
    key_tiles = key_tiles.reshape(tile_count, BLOCK_TOKENS, kv_heads, HEAD_SIZE)
    value_tiles = jnp.concatenate([value_heads] + [shifted[1] for shifted in earlier], axis=0)
    value_tiles = value_tiles.reshape(tile_count, BLOCK_TOKENS, kv_heads, HEAD_SIZE)
    group_size = math.gcd(per_window, 4)
    rounds = per_window // group_size
    query_groups = query_heads.reshape(
        rounds, group_size, BLOCK_TOKENS, kv_heads, head_groups, HEAD_SIZE
    )
    grad_groups = grad_heads.reshape(
        rounds, group_size, BLOCK_TOKENS, kv_heads, head_groups, HEAD_SIZE
    )
    tile_groups = tiles.reshape(rounds, group_size, MAXT)
    kind_groups = kinds.reshape(rounds, group_size, MAXT)

    def one_round(totals, inputs):
        summed_key_grad, summed_value_grad = totals
        query_part, grad_part, tile_part, kind_part = inputs
        flat_tiles = tile_part.reshape(group_size * MAXT)
        grad_query, grad_key, grad_value = jax.vmap(block_grads)(
            query_part, grad_part, key_tiles[tile_part], value_tiles[tile_part], kind_part
        )
        summed_key_grad = summed_key_grad.at[flat_tiles].add(
            grad_key.reshape(group_size * MAXT, BLOCK_TOKENS, kv_heads, HEAD_SIZE)
        )
        summed_value_grad = summed_value_grad.at[flat_tiles].add(
            grad_value.reshape(group_size * MAXT, BLOCK_TOKENS, kv_heads, HEAD_SIZE)
        )
        return ((summed_key_grad, summed_value_grad), grad_query)

    blank_total_sum = jnp.zeros((tile_count, BLOCK_TOKENS, kv_heads, HEAD_SIZE), jnp.float32)
    (summed_key_grad, summed_value_grad), grad_queries = lax.scan(
        one_round,
        (blank_total_sum, blank_total_sum),
        (query_groups, grad_groups, tile_groups, kind_groups),
    )
    key_parts = summed_key_grad.reshape(REACH + 1, window, kv_heads * HEAD_SIZE)
    value_parts = summed_value_grad.reshape(REACH + 1, window, kv_heads * HEAD_SIZE)
    moving_sum = (key_parts[REACH], value_parts[REACH])
    for offset in range(REACH - 1, -1, -1):
        arrived = shifted_2((moving_sum[0], moving_sum[1]), "tm", -1)
        moving_sum = (arrived[0] + key_parts[offset], arrived[1] + value_parts[offset])
    key_total, value_total = moving_sum
    grad_query_heads = grad_queries.reshape(window, head_groups * kv_heads * HEAD_SIZE)
    return (
        lax.all_to_all(grad_query_heads, "space", split_axis=0, concat_axis=1, tiled=True),
        lax.all_to_all(
            key_total.astype(jnp.bfloat16), "space", split_axis=0, concat_axis=1, tiled=True
        ),
        lax.all_to_all(
            value_total.astype(jnp.bfloat16), "space", split_axis=0, concat_axis=1, tiled=True
        ),
    )


def packed(arrays, half, first, width):
    start = half * (arrays[0].shape[1] // 2) + first
    return jnp.concatenate([lax.dynamic_slice_in_dim(a, start, width, 1) for a in arrays], axis=0)


def dot(a, b, contract):
    return lax.dot_general(a, b, ((contract[:1], contract[1:]), ((), ())), preferred_element_type=jnp.float32)


def find_limits(side, code_ref, limit_ref):
    for r in range(2):
        block = side if r == 0 else 1 - side
        codes = [code_ref[block * MAXT + m] for m in range(MAXT)]
        for p in range(2 * (REACH + 1)):
            value = p // 2 * 2 + (side if p % 2 == 0 else 1 - side)
            limit = -FAR
            for code in codes:
                limit = jnp.where(code == 4 * value, FAR, jnp.where(code == 4 * value + 1, 0, limit))
            limit_ref[r * 6 + p] = limit


def attend_kernel(
    side_ref, code_ref,
    q_own, g_own, qg_other, k_own, v_own, kv_other, kv2_own, kv2_other, kv1,
    dq_own, dq_other, d0_own, d0_other, d1_own, d1_other, d2_own, d2_other,
    limit_ref, *scratch,
):
    n, d = BLOCK_TOKENS, HEAD_SIZE

    @pl.when(pl.program_id(0) == 0)
    def _():
        find_limits(side_ref[0], code_ref, limit_ref)

    lanes = 2 * n
    column = lax.broadcasted_iota(jnp.int32, (n, lanes), 0)
    row = lax.broadcasted_iota(jnp.int32, (n, lanes), 1)
    ahead = column - jnp.where(row >= n, row - n, row)
    scale = 1.0 / math.sqrt(d)
    rate = scale * math.log2(math.e)
    for h in range(STEP_HEADS):
        q_all, g_all, k_all, v_all, s_ref, dp_ref, p_ref, ds_ref = scratch[8 * h : 8 * h + 8]
        wide, slim = slice(2 * h * d, 2 * (h + 1) * d), slice(h * d, (h + 1) * d)
        for r, (q, g) in enumerate(
            ((q_own[:, wide], g_own[:, wide]), (qg_other[:n, wide], qg_other[n:, wide]))
        ):
            for j in range(2):
                rows = slice((2 * r + j) * n, (2 * r + j + 1) * n)
                q_all[rows, :] = q[:, j * d : (j + 1) * d]
                g_all[rows, :] = g[:, j * d : (j + 1) * d]
        tiles = (
            (k_own[:, slim], v_own[:, slim]),
            (kv_other[:n, slim], kv_other[n:, slim]),
            (kv1[:n, slim], kv1[n : 2 * n, slim]),
            (kv1[2 * n : 3 * n, slim], kv1[3 * n :, slim]),
            (kv2_own[:n, slim], kv2_own[n:, slim]),
            (kv2_other[:n, slim], kv2_other[n:, slim]),
        )
        for p, (k, v) in enumerate(tiles):
            k_all[p * n : (p + 1) * n, :] = k
            v_all[p * n : (p + 1) * n, :] = v
        for r in range(2):
            cols = slice(r * lanes, (r + 1) * lanes)
            q, g = q_all[cols, :], g_all[cols, :]
            top = None
            for p in range(6):
                rows = slice(p * n, (p + 1) * n)
                s = dot(k_all[rows, :], q, (1, 1))
                s = jnp.where(ahead <= limit_ref[r * 6 + p], s, HIDDEN)
                s_ref[rows, :] = s
                high = jnp.max(s.reshape(n // 8, 8, lanes), axis=0)
                top = high if top is None else jnp.maximum(top, high)
            top = jnp.max(top, axis=0, keepdims=True)
            total = jnp.zeros((8, lanes), jnp.float32)
            delta = jnp.zeros((8, lanes), jnp.float32)
            for p in range(6):
                rows = slice(p * n, (p + 1) * n)
                e = jnp.exp2((s_ref[rows, :] - top) * rate)
                dp = dot(v_all[rows, :], g, (1, 1))
                s_ref[rows, :] = e
                dp_ref[rows, :] = dp
                total = total + jnp.sum(e.reshape(n // 8, 8, lanes), axis=0)
                delta = delta + jnp.sum((e * dp).reshape(n // 8, 8, lanes), axis=0)
            share = 1.0 / jnp.sum(total, axis=0, keepdims=True)
            delta = jnp.sum(delta, axis=0, keepdims=True) * share
            for p in range(6):
                rows = slice(p * n, (p + 1) * n)
                prob = s_ref[rows, :] * share
                ds = prob * (dp_ref[rows, :] - delta)
                p_ref[rows, cols] = prob.astype(jnp.bfloat16)
                ds_ref[rows, cols] = ds.astype(jnp.bfloat16)
        dk = dot(ds_ref[...], q_all[...], (1, 0)) * scale
        dv = dot(p_ref[...], g_all[...], (1, 0))
        for p, out in enumerate((d0_own, d0_other, d1_own, d1_other, d2_own, d2_other)):
            rows = slice(p * n, (p + 1) * n)
            out[:n, slim] = dk[rows].astype(out.dtype)
            out[n:, slim] = dv[rows].astype(out.dtype)
        dq = (dot(k_all[...], ds_ref[...], (0, 0)) * scale).T.astype(jnp.bfloat16)
        for j in range(2):
            here = slice((2 * h + j) * d, (2 * h + j + 1) * d)
            dq_own[:, here] = dq[j * n : (j + 1) * n, :]
            dq_other[:, here] = dq[(2 + j) * n : (3 + j) * n, :]


def attend(side, limits, first, heads, queries, grads, keys, values, qg_other, kv_other, kv2_own, kv2_other, kv1):
    n, d = BLOCK_TOKENS, HEAD_SIZE
    steps = heads // STEP_HEADS
    per_side = keys.shape[1] // (2 * d * STEP_HEADS)
    slim, wide = STEP_HEADS * d, 2 * STEP_HEADS * d

    def mine(h, side_ref, code_ref):
        return 0, side_ref[0] * per_side + first // STEP_HEADS + h

    def here(h, side_ref, code_ref):
        return 0, h

    def out(rows, width, dtype):
        return (
            jax.ShapeDtypeStruct((rows, steps * width), dtype),
            pl.BlockSpec((rows, width), here),
        )

    outs = [
        out(n, wide, jnp.bfloat16),
        out(n, wide, jnp.bfloat16),
        out(2 * n, slim, jnp.float32),
        out(2 * n, slim, jnp.float32),
        out(2 * n, slim, jnp.bfloat16),
        out(2 * n, slim, jnp.bfloat16),
        out(2 * n, slim, jnp.bfloat16),
        out(2 * n, slim, jnp.bfloat16),
    ]
    work = [
        pltpu.VMEM((4 * n, d), jnp.bfloat16),
        pltpu.VMEM((4 * n, d), jnp.bfloat16),
        pltpu.VMEM((6 * n, d), jnp.bfloat16),
        pltpu.VMEM((6 * n, d), jnp.bfloat16),
        pltpu.VMEM((6 * n, 2 * n), jnp.float32),
        pltpu.VMEM((6 * n, 2 * n), jnp.float32),
        pltpu.VMEM((6 * n, 4 * n), jnp.bfloat16),
        pltpu.VMEM((6 * n, 4 * n), jnp.bfloat16),
    ]
    return pl.pallas_call(
        attend_kernel,
        grid_spec=pltpu.PrefetchScalarGridSpec(
            num_scalar_prefetch=2,
            grid=(steps,),
            in_specs=[
                pl.BlockSpec((n, wide), mine),
                pl.BlockSpec((n, wide), mine),
                pl.BlockSpec((2 * n, wide), here),
                pl.BlockSpec((n, slim), mine),
                pl.BlockSpec((n, slim), mine),
                pl.BlockSpec((2 * n, slim), here),
                pl.BlockSpec((2 * n, slim), here),
                pl.BlockSpec((2 * n, slim), here),
                pl.BlockSpec((4 * n, slim), here),
            ],
            out_specs=[spec for _, spec in outs],
            scratch_shapes=[pltpu.SMEM((12,), jnp.int32)] + work * STEP_HEADS,
        ),
        out_shape=[shape for shape, _ in outs],
        compiler_params=pltpu.CompilerParams(vmem_limit_bytes=VMEM_BYTES),
    )(side, limits, queries, grads, qg_other, keys, values, kv_other, kv2_own, kv2_other, kv1)


def swap(block):
    return lax.ppermute(block, "space", [(0, 1), (1, 0)])


def mate(block):
    return lax.ppermute(block, "tm", [(i, i ^ 1) for i in range(lax.axis_size("tm"))])


def moved(block, distance):
    size = lax.axis_size("tm")
    return lax.ppermute(
        block, "tm", [(i, i + distance) for i in range(size) if 0 <= i + distance < size]
    )


def after(arrays, *earlier):
    arrays = list(arrays)
    return lax.optimization_barrier((*arrays, *earlier))[: len(arrays)]


def pair_body(queries, keys, values, output_gradient, tiles, kinds):
    n, d = BLOCK_TOKENS, HEAD_SIZE
    side = lax.axis_index("space")
    odd = lax.axis_index("tm") % 2 == 1
    half = keys.shape[1] // (2 * d)
    sizes = [half // 2, half - half // 2]
    firsts = [0, half // 2]
    place = side.reshape(1).astype(jnp.int32)
    codes = 4 * tiles + kinds
    limits = jnp.concatenate([codes[0], codes[1]])

    def kv_part(part, c, *earlier):
        return packed(after([keys, values], *earlier), part, firsts[c] * d, sizes[c] * d)

    def qg_part(part, c, *earlier):
        arrays = after([queries, output_gradient], *earlier)
        return packed(arrays, part, 2 * firsts[c] * d, 2 * sizes[c] * d)

    kv_away = [kv_part(1 - side, 0)]
    kv_away.append(kv_part(1 - side, 1, kv_away[0]))
    kv_own = [kv_part(side, 0, kv_away[1])]
    qg_away = [qg_part(1 - side, 0, kv_own[0])]
    qg_away.append(qg_part(1 - side, 1, qg_away[0]))
    kv_own.append(kv_part(side, 1, qg_away[1]))

    kv_other = [swap(b) for b in kv_away]
    qg_other = [swap(b) for b in qg_away]
    kv2_own, kv2_other = [moved(kv_own[0], 2)], [moved(kv_other[0], 2)]
    late = moved(jnp.concatenate([kv_own[1], kv_other[1]], axis=0), 2)
    kv2_own.append(late[: 2 * n])
    kv2_other.append(late[2 * n :])

    def attended(c, *earlier):
        if earlier:
            kv2_own[c], kv2_other[c] = after([kv2_own[c], kv2_other[c]], e1_own, e1_other)
        kv1 = mate(
            jnp.concatenate(
                [
                    jnp.where(odd, kv2_own[c], kv_own[c]),
                    jnp.where(odd, kv2_other[c], kv_other[c]),
                ],
                axis=0,
            )
        )
        return attend(
            place, after([limits], *earlier)[0] if earlier else limits, firsts[c], sizes[c],
            queries, output_gradient, keys, values,
            qg_other[c], kv_other[c], kv2_own[c], kv2_other[c], kv1,
        )

    def low(total):
        return total.astype(jnp.bfloat16)

    def back_sum(own, met):
        return low(own + jnp.where(odd, met.astype(jnp.float32), 0.0))

    def here_sum(own, met, back):
        return low(own + jnp.where(odd, 0.0, met.astype(jnp.float32)) + back)

    dq_own0, dq_away0, e0_own, e0_other, e1_own, e1_other, e2_own, e2_other = attended(0)
    e1_own, e1_other = after([e1_own, e1_other], qg_other[1])
    dq_other0 = swap(dq_away0)
    e1_own, e1_other = mate(e1_own), mate(e1_other)
    ship0 = [jnp.concatenate([back_sum(e2_own, e1_own), back_sum(e2_other, e1_other)], axis=0)]
    back0 = moved(ship0[0], -2)
    back_own0, back_other0 = back0[: 2 * n], back0[2 * n :]

    dq_own1, dq_away1, d0_own, d0_other, d1_own, d1_other, d2_own, d2_other = attended(1, *ship0)
    dq_other1 = swap(dq_away1)
    d1_other = mate(d1_other)
    d1_own = mate(d1_own)
    d1_other, back_other0 = after([d1_other, back_other0])
    ship_other = back_sum(d2_other, d1_other)
    back_other = moved(ship_other, -2)
    ship_own = back_sum(d2_own, d1_own)
    back_own = moved(ship_own, -2)
    (back_other0,) = after([back_other0], ship_other)
    other0 = swap(here_sum(e0_other, e1_other, back_other0))
    other1 = swap(here_sum(d0_other, d1_other, back_other))
    own0 = here_sum(e0_own, e1_own, back_own0)
    own1 = here_sum(d0_own, d1_own, back_own)

    def placed(own, other):
        own, other = jnp.concatenate(own, axis=1), jnp.concatenate(other, axis=1)
        return jnp.where(
            side == 0,
            jnp.concatenate([own, other], axis=1),
            jnp.concatenate([other, own], axis=1),
        )

    dq_own0, dq_own1, dq_other0, dq_other1 = after(
        [dq_own0, dq_own1, dq_other0, dq_other1], ship_other, ship_own
    )
    grad_queries = placed([dq_own0, dq_own1], [dq_other0, dq_other1])
    blank = jnp.zeros_like(own1[:n])
    grad_keys = placed([own0[:n], own1[:n]], [other0[:n], blank])
    grad_values = placed([own0[n:], own1[n:]], [other0[n:], blank])
    grad_keys, grad_values, other1 = after([grad_keys, grad_values, other1])
    last = ((1 - side) * half + firsts[1]) * d
    return (
        grad_queries,
        lax.dynamic_update_slice_in_dim(grad_keys, other1[:n], last, 1),
        lax.dynamic_update_slice_in_dim(grad_values, other1[n:], last, 1),
    )


def body(queries, keys, values, output_gradient, tiles, kinds):
    pair = (
        lax.axis_size("space") == 2
        and lax.axis_size("tm") % 2 == 0
        and tiles.shape[0] == 2
        and queries.shape[0] == BLOCK_TOKENS
        and queries.shape[1] == 2 * keys.shape[1]
        and keys.shape[1] % (4 * HEAD_SIZE) == 0
    )
    run = pair_body if pair else general_body
    return run(queries, keys, values, output_gradient, tiles, kinds)


def solution(mesh):
    in_specs = (
        P(("tm", "space"), None),
        P(("tm", "space"), None),
        P(("tm", "space"), None),
        P(("tm", "space"), None),
        P("tm", None),
        P("tm", None),
    )
    out_specs = (P(("tm", "space"), None), P(("tm", "space"), None), P(("tm", "space"), None))
    return jax.shard_map(body, mesh=mesh, in_specs=in_specs, out_specs=out_specs, check_vma=False)
```

```python
import math

import jax
import jax.numpy as jnp
from jax import lax
from jax.experimental import pallas as pl
from jax.experimental.pallas import tpu as pltpu
from jax.sharding import PartitionSpec as P

HEAD_SIZE = 128
BLOCK_TOKENS = 128
MAXT = 6
REACH = 2
STEP_HEADS = 1
HIDDEN = -1e30
FAR = 1 << 20
VMEM_BYTES = 53248 * 1024


def shifted_2(block, axis, distance):
    devices = range(lax.axis_size(axis))
    route = [(i - distance, i) for i in devices if i - distance in devices]
    return lax.ppermute(block, axis, route)


def block_grads(query_rows, grad_rows, key_tiles, value_tiles, tile_kinds):
    blocks, length, kv_count, head_dim = key_tiles.shape
    score_scale = 1.0 / head_dim**0.5
    key_flat = key_tiles.reshape(blocks * length, kv_count, head_dim)
    value_flat = value_tiles.reshape(blocks * length, kv_count, head_dim)
    scores = (
        jnp.einsum("qkgd,tkd->kgqt", query_rows, key_flat, preferred_element_type=jnp.float32)
        * score_scale
    )
    query_pos = jnp.arange(length)
    column_kind = jnp.repeat(tile_kinds, length)
    column_pos = jnp.tile(jnp.arange(length), blocks)
    visible = (column_kind == 0)[None, :] | (column_kind == 1)[None, :] & (
        column_pos[None, :] <= query_pos[:, None]
    )
    masked = jnp.where(visible, scores, -jnp.inf)
    row_max = jnp.max(masked, axis=-1, keepdims=True)
    weights = jnp.where(visible, jnp.exp(masked - row_max), 0.0)
    probabilities = weights / jnp.sum(weights, axis=-1, keepdims=True)
    probs_low = probabilities.astype(jnp.bfloat16)
    outputs = jnp.einsum(
        "kgqt,tkd->qkgd", probs_low, value_flat, preferred_element_type=jnp.float32
    )
    row_delta = jnp.einsum("qkgd,qkgd->kgq", grad_rows.astype(jnp.float32), outputs)
    grad_probs = jnp.einsum(
        "qkgd,tkd->kgqt", grad_rows, value_flat, preferred_element_type=jnp.float32
    )
    grad_scores = (score_scale * probabilities * (grad_probs - row_delta[..., None])).astype(
        jnp.bfloat16
    )
    grad_query = jnp.einsum(
        "kgqt,tkd->qkgd", grad_scores, key_flat, preferred_element_type=jnp.float32
    )
    grad_key = jnp.einsum(
        "kgqt,qkgd->tkd", grad_scores, query_rows, preferred_element_type=jnp.float32
    )
    grad_value = jnp.einsum(
        "kgqt,qkgd->tkd", probs_low, grad_rows, preferred_element_type=jnp.float32
    )
    return (
        grad_query.astype(jnp.bfloat16),
        grad_key.reshape(blocks, length, kv_count, head_dim),
        grad_value.reshape(blocks, length, kv_count, head_dim),
    )


def general_body(queries, keys, values, output_gradient, tiles, kinds):
    query_heads, grad_heads, key_heads, value_heads = (
        lax.all_to_all(queries, "space", split_axis=1, concat_axis=0, tiled=True),
        lax.all_to_all(output_gradient, "space", split_axis=1, concat_axis=0, tiled=True),
        lax.all_to_all(keys, "space", split_axis=1, concat_axis=0, tiled=True),
        lax.all_to_all(values, "space", split_axis=1, concat_axis=0, tiled=True),
    )
    window = query_heads.shape[0]
    kv_heads = key_heads.shape[1] // HEAD_SIZE
    head_groups = query_heads.shape[1] // key_heads.shape[1]
    per_window = window // BLOCK_TOKENS
    earlier = [shifted_2((key_heads, value_heads), "tm", offset) for offset in range(1, REACH + 1)]
    tile_count = (REACH + 1) * per_window
    key_tiles = jnp.concatenate([key_heads] + [shifted[0] for shifted in earlier], axis=0)
    key_tiles = key_tiles.reshape(tile_count, BLOCK_TOKENS, kv_heads, HEAD_SIZE)
    value_tiles = jnp.concatenate([value_heads] + [shifted[1] for shifted in earlier], axis=0)
    value_tiles = value_tiles.reshape(tile_count, BLOCK_TOKENS, kv_heads, HEAD_SIZE)
    group_size = math.gcd(per_window, 4)
    rounds = per_window // group_size
    query_groups = query_heads.reshape(
        rounds, group_size, BLOCK_TOKENS, kv_heads, head_groups, HEAD_SIZE
    )
    grad_groups = grad_heads.reshape(
        rounds, group_size, BLOCK_TOKENS, kv_heads, head_groups, HEAD_SIZE
    )
    tile_groups = tiles.reshape(rounds, group_size, MAXT)
    kind_groups = kinds.reshape(rounds, group_size, MAXT)

    def one_round(totals, inputs):
        summed_key_grad, summed_value_grad = totals
        query_part, grad_part, tile_part, kind_part = inputs
        flat_tiles = tile_part.reshape(group_size * MAXT)
        grad_query, grad_key, grad_value = jax.vmap(block_grads)(
            query_part, grad_part, key_tiles[tile_part], value_tiles[tile_part], kind_part
        )
        summed_key_grad = summed_key_grad.at[flat_tiles].add(
            grad_key.reshape(group_size * MAXT, BLOCK_TOKENS, kv_heads, HEAD_SIZE)
        )
        summed_value_grad = summed_value_grad.at[flat_tiles].add(
            grad_value.reshape(group_size * MAXT, BLOCK_TOKENS, kv_heads, HEAD_SIZE)
        )
        return ((summed_key_grad, summed_value_grad), grad_query)

    blank_total_sum = jnp.zeros((tile_count, BLOCK_TOKENS, kv_heads, HEAD_SIZE), jnp.float32)
    (summed_key_grad, summed_value_grad), grad_queries = lax.scan(
        one_round,
        (blank_total_sum, blank_total_sum),
        (query_groups, grad_groups, tile_groups, kind_groups),
    )
    key_parts = summed_key_grad.reshape(REACH + 1, window, kv_heads * HEAD_SIZE)
    value_parts = summed_value_grad.reshape(REACH + 1, window, kv_heads * HEAD_SIZE)
    moving_sum = (key_parts[REACH], value_parts[REACH])
    for offset in range(REACH - 1, -1, -1):
        arrived = shifted_2((moving_sum[0], moving_sum[1]), "tm", -1)
        moving_sum = (arrived[0] + key_parts[offset], arrived[1] + value_parts[offset])
    key_total, value_total = moving_sum
    grad_query_heads = grad_queries.reshape(window, head_groups * kv_heads * HEAD_SIZE)
    return (
        lax.all_to_all(grad_query_heads, "space", split_axis=0, concat_axis=1, tiled=True),
        lax.all_to_all(
            key_total.astype(jnp.bfloat16), "space", split_axis=0, concat_axis=1, tiled=True
        ),
        lax.all_to_all(
            value_total.astype(jnp.bfloat16), "space", split_axis=0, concat_axis=1, tiled=True
        ),
    )


def packed(arrays, half, first, width):
    start = half * (arrays[0].shape[1] // 2) + first
    return jnp.concatenate([lax.dynamic_slice_in_dim(a, start, width, 1) for a in arrays], axis=0)


def dot(a, b, contract):
    return lax.dot_general(a, b, ((contract[:1], contract[1:]), ((), ())), preferred_element_type=jnp.float32)


def find_limits(side, code_ref, limit_ref):
    for r in range(2):
        block = side if r == 0 else 1 - side
        codes = [code_ref[block * MAXT + m] for m in range(MAXT)]
        for p in range(2 * (REACH + 1)):
            value = p // 2 * 2 + (side if p % 2 == 0 else 1 - side)
            limit = -FAR
            for code in codes:
                limit = jnp.where(code == 4 * value, FAR, jnp.where(code == 4 * value + 1, 0, limit))
            limit_ref[r * 6 + p] = limit


def attend_kernel(
    side_ref, code_ref,
    q_own, g_own, qg_other, k_own, v_own, kv_other, kv2_own, kv2_other, kv1,
    dq_own, dq_other, d0_own, d0_other, d1_own, d1_other, d2_own, d2_other,
    limit_ref, *scratch,
):
    n, d = BLOCK_TOKENS, HEAD_SIZE

    @pl.when(pl.program_id(0) == 0)
    def _():
        find_limits(side_ref[0], code_ref, limit_ref)

    lanes = 2 * n
    column = lax.broadcasted_iota(jnp.int32, (n, lanes), 0)
    row = lax.broadcasted_iota(jnp.int32, (n, lanes), 1)
    ahead = column - jnp.where(row >= n, row - n, row)
    scale = 1.0 / math.sqrt(d)
    rate = scale * math.log2(math.e)
    for h in range(STEP_HEADS):
        q_all, g_all, k_all, v_all, s_ref, dp_ref, p_ref, ds_ref = scratch[8 * h : 8 * h + 8]
        wide, slim = slice(2 * h * d, 2 * (h + 1) * d), slice(h * d, (h + 1) * d)
        for r, (q, g) in enumerate(
            ((q_own[:, wide], g_own[:, wide]), (qg_other[:n, wide], qg_other[n:, wide]))
        ):
            for j in range(2):
                rows = slice((2 * r + j) * n, (2 * r + j + 1) * n)
                q_all[rows, :] = q[:, j * d : (j + 1) * d]
                g_all[rows, :] = g[:, j * d : (j + 1) * d]
        tiles = (
            (k_own[:, slim], v_own[:, slim]),
            (kv_other[:n, slim], kv_other[n:, slim]),
            (kv1[:n, slim], kv1[n : 2 * n, slim]),
            (kv1[2 * n : 3 * n, slim], kv1[3 * n :, slim]),
            (kv2_own[:n, slim], kv2_own[n:, slim]),
            (kv2_other[:n, slim], kv2_other[n:, slim]),
        )
        for p, (k, v) in enumerate(tiles):
            k_all[p * n : (p + 1) * n, :] = k
            v_all[p * n : (p + 1) * n, :] = v
        for r in range(2):
            cols = slice(r * lanes, (r + 1) * lanes)
            q, g = q_all[cols, :], g_all[cols, :]
            top = None
            for p in range(6):
                rows = slice(p * n, (p + 1) * n)
                s = dot(k_all[rows, :], q, (1, 1))
                s = jnp.where(ahead <= limit_ref[r * 6 + p], s, HIDDEN)
                s_ref[rows, :] = s
                high = jnp.max(s.reshape(n // 8, 8, lanes), axis=0)
                top = high if top is None else jnp.maximum(top, high)
            top = jnp.max(top, axis=0, keepdims=True)
            total = jnp.zeros((8, lanes), jnp.float32)
            delta = jnp.zeros((8, lanes), jnp.float32)
            for p in range(6):
                rows = slice(p * n, (p + 1) * n)
                e = jnp.exp2((s_ref[rows, :] - top) * rate)
                dp = dot(v_all[rows, :], g, (1, 1))
                s_ref[rows, :] = e
                dp_ref[rows, :] = dp
                total = total + jnp.sum(e.reshape(n // 8, 8, lanes), axis=0)
                delta = delta + jnp.sum((e * dp).reshape(n // 8, 8, lanes), axis=0)
            share = 1.0 / jnp.sum(total, axis=0, keepdims=True)
            delta = jnp.sum(delta, axis=0, keepdims=True) * share
            for p in range(6):
                rows = slice(p * n, (p + 1) * n)
                prob = s_ref[rows, :] * share
                ds = prob * (dp_ref[rows, :] - delta)
                p_ref[rows, cols] = prob.astype(jnp.bfloat16)
                ds_ref[rows, cols] = ds.astype(jnp.bfloat16)
        dk = dot(ds_ref[...], q_all[...], (1, 0)) * scale
        dv = dot(p_ref[...], g_all[...], (1, 0))
        for p, out in enumerate((d0_own, d0_other, d1_own, d1_other, d2_own, d2_other)):
            rows = slice(p * n, (p + 1) * n)
            out[:n, slim] = dk[rows].astype(out.dtype)
            out[n:, slim] = dv[rows].astype(out.dtype)
        dq = (dot(k_all[...], ds_ref[...], (0, 0)) * scale).T.astype(jnp.bfloat16)
        for j in range(2):
            here = slice((2 * h + j) * d, (2 * h + j + 1) * d)
            dq_own[:, here] = dq[j * n : (j + 1) * n, :]
            dq_other[:, here] = dq[(2 + j) * n : (3 + j) * n, :]


def attend(side, limits, first, heads, queries, grads, keys, values, qg_other, kv_other, kv2_own, kv2_other, kv1):
    n, d = BLOCK_TOKENS, HEAD_SIZE
    steps = heads // STEP_HEADS
    per_side = keys.shape[1] // (2 * d * STEP_HEADS)
    slim, wide = STEP_HEADS * d, 2 * STEP_HEADS * d

    def mine(h, side_ref, code_ref):
        return 0, side_ref[0] * per_side + first // STEP_HEADS + h

    def here(h, side_ref, code_ref):
        return 0, h

    def out(rows, width, dtype):
        return (
            jax.ShapeDtypeStruct((rows, steps * width), dtype),
            pl.BlockSpec((rows, width), here),
        )

    outs = [
        out(n, wide, jnp.bfloat16),
        out(n, wide, jnp.bfloat16),
        out(2 * n, slim, jnp.float32),
        out(2 * n, slim, jnp.float32),
        out(2 * n, slim, jnp.bfloat16),
        out(2 * n, slim, jnp.bfloat16),
        out(2 * n, slim, jnp.bfloat16),
        out(2 * n, slim, jnp.bfloat16),
    ]
    work = [
        pltpu.VMEM((4 * n, d), jnp.bfloat16),
        pltpu.VMEM((4 * n, d), jnp.bfloat16),
        pltpu.VMEM((6 * n, d), jnp.bfloat16),
        pltpu.VMEM((6 * n, d), jnp.bfloat16),
        pltpu.VMEM((6 * n, 2 * n), jnp.float32),
        pltpu.VMEM((6 * n, 2 * n), jnp.float32),
        pltpu.VMEM((6 * n, 4 * n), jnp.bfloat16),
        pltpu.VMEM((6 * n, 4 * n), jnp.bfloat16),
    ]
    return pl.pallas_call(
        attend_kernel,
        grid_spec=pltpu.PrefetchScalarGridSpec(
            num_scalar_prefetch=2,
            grid=(steps,),
            in_specs=[
                pl.BlockSpec((n, wide), mine),
                pl.BlockSpec((n, wide), mine),
                pl.BlockSpec((2 * n, wide), here),
                pl.BlockSpec((n, slim), mine),
                pl.BlockSpec((n, slim), mine),
                pl.BlockSpec((2 * n, slim), here),
                pl.BlockSpec((2 * n, slim), here),
                pl.BlockSpec((2 * n, slim), here),
                pl.BlockSpec((4 * n, slim), here),
            ],
            out_specs=[spec for _, spec in outs],
            scratch_shapes=[pltpu.SMEM((12,), jnp.int32)] + work * STEP_HEADS,
        ),
        out_shape=[shape for shape, _ in outs],
        compiler_params=pltpu.CompilerParams(vmem_limit_bytes=VMEM_BYTES),
    )(side, limits, queries, grads, qg_other, keys, values, kv_other, kv2_own, kv2_other, kv1)


def swap(block):
    return lax.ppermute(block, "space", [(0, 1), (1, 0)])


def mate(block):
    return lax.ppermute(block, "tm", [(i, i ^ 1) for i in range(lax.axis_size("tm"))])


def moved(block, distance):
    size = lax.axis_size("tm")
    return lax.ppermute(
        block, "tm", [(i, i + distance) for i in range(size) if 0 <= i + distance < size]
    )


def after(arrays, *earlier):
    arrays = list(arrays)
    return lax.optimization_barrier((*arrays, *earlier))[: len(arrays)]


def pair_body(queries, keys, values, output_gradient, tiles, kinds):
    n, d = BLOCK_TOKENS, HEAD_SIZE
    side = lax.axis_index("space")
    odd = lax.axis_index("tm") % 2 == 1
    half = keys.shape[1] // (2 * d)
    sizes = [half // 2, half - half // 2]
    firsts = [0, half // 2]
    place = side.reshape(1).astype(jnp.int32)
    codes = 4 * tiles + kinds
    limits = jnp.concatenate([codes[0], codes[1]])

    def kv_part(part, c, *earlier):
        return packed(after([keys, values], *earlier), part, firsts[c] * d, sizes[c] * d)

    def qg_part(part, c, *earlier):
        arrays = after([queries, output_gradient], *earlier)
        return packed(arrays, part, 2 * firsts[c] * d, 2 * sizes[c] * d)

    kv_away = [kv_part(1 - side, 0)]
    kv_away.append(kv_part(1 - side, 1, kv_away[0]))
    kv_own = [kv_part(side, 0, kv_away[1])]
    qg_away = [qg_part(1 - side, 0, kv_own[0])]
    qg_away.append(qg_part(1 - side, 1, qg_away[0]))
    kv_own.append(kv_part(side, 1, qg_away[1]))

    kv_other = [swap(b) for b in kv_away]
    qg_other = [swap(b) for b in qg_away]
    kv2_own, kv2_other = [moved(kv_own[0], 2)], [moved(kv_other[0], 2)]
    late = moved(jnp.concatenate([kv_own[1], kv_other[1]], axis=0), 2)
    kv2_own.append(late[: 2 * n])
    kv2_other.append(late[2 * n :])

    def attended(c, *earlier):
        if earlier:
            kv2_own[c], kv2_other[c] = after([kv2_own[c], kv2_other[c]], e1_own, e1_other)
        kv1 = mate(
            jnp.concatenate(
                [
                    jnp.where(odd, kv2_own[c], kv_own[c]),
                    jnp.where(odd, kv2_other[c], kv_other[c]),
                ],
                axis=0,
            )
        )
        return attend(
            place, after([limits], *earlier)[0] if earlier else limits, firsts[c], sizes[c],
            queries, output_gradient, keys, values,
            qg_other[c], kv_other[c], kv2_own[c], kv2_other[c], kv1,
        )

    def low(total):
        return total.astype(jnp.bfloat16)

    def back_sum(own, met):
        return low(own + jnp.where(odd, met.astype(jnp.float32), 0.0))

    def here_sum(own, met, back):
        return low(own + jnp.where(odd, 0.0, met.astype(jnp.float32)) + back)

    dq_own0, dq_away0, e0_own, e0_other, e1_own, e1_other, e2_own, e2_other = attended(0)
    e1_own, e1_other = after([e1_own, e1_other], qg_other[1])
    dq_other0 = swap(dq_away0)
    e1_own, e1_other = mate(e1_own), mate(e1_other)
    ship0 = [jnp.concatenate([back_sum(e2_own, e1_own), back_sum(e2_other, e1_other)], axis=0)]
    back0 = moved(ship0[0], -2)
    back_own0, back_other0 = back0[: 2 * n], back0[2 * n :]

    dq_own1, dq_away1, d0_own, d0_other, d1_own, d1_other, d2_own, d2_other = attended(1, *ship0)
    dq_other1 = swap(dq_away1)
    d1_other = mate(d1_other)
    d1_own = mate(d1_own)
    d1_other, back_other0 = after([d1_other, back_other0])
    ship_other = back_sum(d2_other, d1_other)
    back_other = moved(ship_other, -2)
    ship_own = back_sum(d2_own, d1_own)
    back_own = moved(ship_own, -2)
    (back_other0,) = after([back_other0], ship_other)
    other0 = swap(here_sum(e0_other, e1_other, back_other0))
    other1 = swap(here_sum(d0_other, d1_other, back_other))
    own0 = here_sum(e0_own, e1_own, back_own0)
    own1 = here_sum(d0_own, d1_own, back_own)

    def placed(own, other):
        own, other = jnp.concatenate(own, axis=1), jnp.concatenate(other, axis=1)
        return jnp.where(
            side == 0,
            jnp.concatenate([own, other], axis=1),
            jnp.concatenate([other, own], axis=1),
        )

    dq_own0, dq_own1, dq_other0, dq_other1 = after(
        [dq_own0, dq_own1, dq_other0, dq_other1], ship_other, ship_own
    )
    grad_queries = placed([dq_own0, dq_own1], [dq_other0, dq_other1])
    blank = jnp.zeros_like(own1[:n])
    grad_keys = placed([own0[:n], own1[:n]], [other0[:n], blank])
    grad_values = placed([own0[n:], own1[n:]], [other0[n:], blank])
    grad_keys, grad_values, other1 = after([grad_keys, grad_values, other1])
    last = ((1 - side) * half + firsts[1]) * d
    return (
        grad_queries,
        lax.dynamic_update_slice_in_dim(grad_keys, other1[:n], last, 1),
        lax.dynamic_update_slice_in_dim(grad_values, other1[n:], last, 1),
    )


def body(queries, keys, values, output_gradient, tiles, kinds):
    pair = (
        lax.axis_size("space") == 2
        and lax.axis_size("tm") % 2 == 0
        and tiles.shape[0] == 2
        and queries.shape[0] == BLOCK_TOKENS
        and queries.shape[1] == 2 * keys.shape[1]
        and keys.shape[1] % (4 * HEAD_SIZE) == 0
    )
    run = pair_body if pair else general_body
    return run(queries, keys, values, output_gradient, tiles, kinds)


def solution(mesh):
    in_specs = (
        P(("tm", "space"), None),
        P(("tm", "space"), None),
        P(("tm", "space"), None),
        P(("tm", "space"), None),
        P("tm", None),
        P("tm", None),
    )
    out_specs = (P(("tm", "space"), None), P(("tm", "space"), None), P(("tm", "space"), None))
    return jax.shard_map(body, mesh=mesh, in_specs=in_specs, out_specs=out_specs, check_vma=False)
```

```python
import math

import jax
import jax.numpy as jnp
from jax import lax
from jax.experimental import pallas as pl
from jax.experimental.pallas import tpu as pltpu
from jax.sharding import PartitionSpec as P

HEAD_SIZE = 128
BLOCK_TOKENS = 128
MAXT = 6
REACH = 2
STEP_HEADS = 2
HIDDEN = -1e30
FAR = 1 << 20
VMEM_BYTES = 53248 * 1024


def shifted_2(block, axis, distance):
    devices = range(lax.axis_size(axis))
    route = [(i - distance, i) for i in devices if i - distance in devices]
    return lax.ppermute(block, axis, route)


def block_grads(query_rows, grad_rows, key_tiles, value_tiles, tile_kinds):
    blocks, length, kv_count, head_dim = key_tiles.shape
    score_scale = 1.0 / head_dim**0.5
    key_flat = key_tiles.reshape(blocks * length, kv_count, head_dim)
    value_flat = value_tiles.reshape(blocks * length, kv_count, head_dim)
    scores = (
        jnp.einsum("qkgd,tkd->kgqt", query_rows, key_flat, preferred_element_type=jnp.float32)
        * score_scale
    )
    query_pos = jnp.arange(length)
    column_kind = jnp.repeat(tile_kinds, length)
    column_pos = jnp.tile(jnp.arange(length), blocks)
    visible = (column_kind == 0)[None, :] | (column_kind == 1)[None, :] & (
        column_pos[None, :] <= query_pos[:, None]
    )
    masked = jnp.where(visible, scores, -jnp.inf)
    row_max = jnp.max(masked, axis=-1, keepdims=True)
    weights = jnp.where(visible, jnp.exp(masked - row_max), 0.0)
    probabilities = weights / jnp.sum(weights, axis=-1, keepdims=True)
    probs_low = probabilities.astype(jnp.bfloat16)
    outputs = jnp.einsum(
        "kgqt,tkd->qkgd", probs_low, value_flat, preferred_element_type=jnp.float32
    )
    row_delta = jnp.einsum("qkgd,qkgd->kgq", grad_rows.astype(jnp.float32), outputs)
    grad_probs = jnp.einsum(
        "qkgd,tkd->kgqt", grad_rows, value_flat, preferred_element_type=jnp.float32
    )
    grad_scores = (score_scale * probabilities * (grad_probs - row_delta[..., None])).astype(
        jnp.bfloat16
    )
    grad_query = jnp.einsum(
        "kgqt,tkd->qkgd", grad_scores, key_flat, preferred_element_type=jnp.float32
    )
    grad_key = jnp.einsum(
        "kgqt,qkgd->tkd", grad_scores, query_rows, preferred_element_type=jnp.float32
    )
    grad_value = jnp.einsum(
        "kgqt,qkgd->tkd", probs_low, grad_rows, preferred_element_type=jnp.float32
    )
    return (
        grad_query.astype(jnp.bfloat16),
        grad_key.reshape(blocks, length, kv_count, head_dim),
        grad_value.reshape(blocks, length, kv_count, head_dim),
    )


def general_body(queries, keys, values, output_gradient, tiles, kinds):
    query_heads, grad_heads, key_heads, value_heads = (
        lax.all_to_all(queries, "space", split_axis=1, concat_axis=0, tiled=True),
        lax.all_to_all(output_gradient, "space", split_axis=1, concat_axis=0, tiled=True),
        lax.all_to_all(keys, "space", split_axis=1, concat_axis=0, tiled=True),
        lax.all_to_all(values, "space", split_axis=1, concat_axis=0, tiled=True),
    )
    window = query_heads.shape[0]
    kv_heads = key_heads.shape[1] // HEAD_SIZE
    head_groups = query_heads.shape[1] // key_heads.shape[1]
    per_window = window // BLOCK_TOKENS
    earlier = [shifted_2((key_heads, value_heads), "tm", offset) for offset in range(1, REACH + 1)]
    tile_count = (REACH + 1) * per_window
    key_tiles = jnp.concatenate([key_heads] + [shifted[0] for shifted in earlier], axis=0)
    key_tiles = key_tiles.reshape(tile_count, BLOCK_TOKENS, kv_heads, HEAD_SIZE)
    value_tiles = jnp.concatenate([value_heads] + [shifted[1] for shifted in earlier], axis=0)
    value_tiles = value_tiles.reshape(tile_count, BLOCK_TOKENS, kv_heads, HEAD_SIZE)
    group_size = math.gcd(per_window, 4)
    rounds = per_window // group_size
    query_groups = query_heads.reshape(
        rounds, group_size, BLOCK_TOKENS, kv_heads, head_groups, HEAD_SIZE
    )
    grad_groups = grad_heads.reshape(
        rounds, group_size, BLOCK_TOKENS, kv_heads, head_groups, HEAD_SIZE
    )
    tile_groups = tiles.reshape(rounds, group_size, MAXT)
    kind_groups = kinds.reshape(rounds, group_size, MAXT)

    def one_round(totals, inputs):
        summed_key_grad, summed_value_grad = totals
        query_part, grad_part, tile_part, kind_part = inputs
        flat_tiles = tile_part.reshape(group_size * MAXT)
        grad_query, grad_key, grad_value = jax.vmap(block_grads)(
            query_part, grad_part, key_tiles[tile_part], value_tiles[tile_part], kind_part
        )
        summed_key_grad = summed_key_grad.at[flat_tiles].add(
            grad_key.reshape(group_size * MAXT, BLOCK_TOKENS, kv_heads, HEAD_SIZE)
        )
        summed_value_grad = summed_value_grad.at[flat_tiles].add(
            grad_value.reshape(group_size * MAXT, BLOCK_TOKENS, kv_heads, HEAD_SIZE)
        )
        return ((summed_key_grad, summed_value_grad), grad_query)

    blank_total_sum = jnp.zeros((tile_count, BLOCK_TOKENS, kv_heads, HEAD_SIZE), jnp.float32)
    (summed_key_grad, summed_value_grad), grad_queries = lax.scan(
        one_round,
        (blank_total_sum, blank_total_sum),
        (query_groups, grad_groups, tile_groups, kind_groups),
    )
    key_parts = summed_key_grad.reshape(REACH + 1, window, kv_heads * HEAD_SIZE)
    value_parts = summed_value_grad.reshape(REACH + 1, window, kv_heads * HEAD_SIZE)
    moving_sum = (key_parts[REACH], value_parts[REACH])
    for offset in range(REACH - 1, -1, -1):
        arrived = shifted_2((moving_sum[0], moving_sum[1]), "tm", -1)
        moving_sum = (arrived[0] + key_parts[offset], arrived[1] + value_parts[offset])
    key_total, value_total = moving_sum
    grad_query_heads = grad_queries.reshape(window, head_groups * kv_heads * HEAD_SIZE)
    return (
        lax.all_to_all(grad_query_heads, "space", split_axis=0, concat_axis=1, tiled=True),
        lax.all_to_all(
            key_total.astype(jnp.bfloat16), "space", split_axis=0, concat_axis=1, tiled=True
        ),
        lax.all_to_all(
            value_total.astype(jnp.bfloat16), "space", split_axis=0, concat_axis=1, tiled=True
        ),
    )


def packed(arrays, half, first, width):
    start = half * (arrays[0].shape[1] // 2) + first
    return jnp.concatenate([lax.dynamic_slice_in_dim(a, start, width, 1) for a in arrays], axis=0)


def dot(a, b, contract):
    return lax.dot_general(a, b, ((contract[:1], contract[1:]), ((), ())), preferred_element_type=jnp.float32)


def find_limits(side, code_ref, limit_ref):
    for r in range(2):
        block = side if r == 0 else 1 - side
        codes = [code_ref[block * MAXT + m] for m in range(MAXT)]
        for p in range(2 * (REACH + 1)):
            value = p // 2 * 2 + (side if p % 2 == 0 else 1 - side)
            limit = -FAR
            for code in codes:
                limit = jnp.where(code == 4 * value, FAR, jnp.where(code == 4 * value + 1, 0, limit))
            limit_ref[r * 6 + p] = limit


def attend_kernel(
    side_ref, code_ref,
    q_own, g_own, qg_other, k_own, v_own, kv_other, kv2_own, kv2_other, kv1,
    dq_own, dq_other, d0_own, d0_other, d1_own, d1_other, d2_own, d2_other,
    limit_ref, *scratch,
):
    n, d = BLOCK_TOKENS, HEAD_SIZE

    @pl.when(pl.program_id(0) == 0)
    def _():
        find_limits(side_ref[0], code_ref, limit_ref)

    lanes = 2 * n
    column = lax.broadcasted_iota(jnp.int32, (n, lanes), 0)
    row = lax.broadcasted_iota(jnp.int32, (n, lanes), 1)
    ahead = column - jnp.where(row >= n, row - n, row)
    scale = 1.0 / math.sqrt(d)
    rate = scale * math.log2(math.e)
    for h in range(STEP_HEADS):
        q_all, g_all, k_all, v_all, s_ref, dp_ref, p_ref, ds_ref = scratch[8 * h : 8 * h + 8]
        wide, slim = slice(2 * h * d, 2 * (h + 1) * d), slice(h * d, (h + 1) * d)
        for r, (q, g) in enumerate(
            ((q_own[:, wide], g_own[:, wide]), (qg_other[:n, wide], qg_other[n:, wide]))
        ):
            for j in range(2):
                rows = slice((2 * r + j) * n, (2 * r + j + 1) * n)
                q_all[rows, :] = q[:, j * d : (j + 1) * d]
                g_all[rows, :] = g[:, j * d : (j + 1) * d]
        tiles = (
            (k_own[:, slim], v_own[:, slim]),
            (kv_other[:n, slim], kv_other[n:, slim]),
            (kv1[:n, slim], kv1[n : 2 * n, slim]),
            (kv1[2 * n : 3 * n, slim], kv1[3 * n :, slim]),
            (kv2_own[:n, slim], kv2_own[n:, slim]),
            (kv2_other[:n, slim], kv2_other[n:, slim]),
        )
        for p, (k, v) in enumerate(tiles):
            k_all[p * n : (p + 1) * n, :] = k
            v_all[p * n : (p + 1) * n, :] = v
        for r in range(2):
            cols = slice(r * lanes, (r + 1) * lanes)
            q, g = q_all[cols, :], g_all[cols, :]
            top = None
            for p in range(6):
                rows = slice(p * n, (p + 1) * n)
                s = dot(k_all[rows, :], q, (1, 1))
                s = jnp.where(ahead <= limit_ref[r * 6 + p], s, HIDDEN)
                s_ref[rows, :] = s
                high = jnp.max(s.reshape(n // 8, 8, lanes), axis=0)
                top = high if top is None else jnp.maximum(top, high)
            top = jnp.max(top, axis=0, keepdims=True)
            total = jnp.zeros((8, lanes), jnp.float32)
            delta = jnp.zeros((8, lanes), jnp.float32)
            for p in range(6):
                rows = slice(p * n, (p + 1) * n)
                e = jnp.exp2((s_ref[rows, :] - top) * rate)
                dp = dot(v_all[rows, :], g, (1, 1))
                s_ref[rows, :] = e
                dp_ref[rows, :] = dp
                total = total + jnp.sum(e.reshape(n // 8, 8, lanes), axis=0)
                delta = delta + jnp.sum((e * dp).reshape(n // 8, 8, lanes), axis=0)
            share = 1.0 / jnp.sum(total, axis=0, keepdims=True)
            delta = jnp.sum(delta, axis=0, keepdims=True) * share
            for p in range(6):
                rows = slice(p * n, (p + 1) * n)
                prob = s_ref[rows, :] * share
                ds = prob * (dp_ref[rows, :] - delta)
                p_ref[rows, cols] = prob.astype(jnp.bfloat16)
                ds_ref[rows, cols] = ds.astype(jnp.bfloat16)
        dk = dot(ds_ref[...], q_all[...], (1, 0)) * scale
        dv = dot(p_ref[...], g_all[...], (1, 0))
        for p, out in enumerate((d0_own, d0_other, d1_own, d1_other, d2_own, d2_other)):
            rows = slice(p * n, (p + 1) * n)
            out[:n, slim] = dk[rows].astype(out.dtype)
            out[n:, slim] = dv[rows].astype(out.dtype)
        dq = (dot(k_all[...], ds_ref[...], (0, 0)) * scale).T.astype(jnp.bfloat16)
        for j in range(2):
            here = slice((2 * h + j) * d, (2 * h + j + 1) * d)
            dq_own[:, here] = dq[j * n : (j + 1) * n, :]
            dq_other[:, here] = dq[(2 + j) * n : (3 + j) * n, :]


def attend(side, limits, first, heads, queries, grads, keys, values, qg_other, kv_other, kv2_own, kv2_other, kv1):
    n, d = BLOCK_TOKENS, HEAD_SIZE
    steps = heads // STEP_HEADS
    per_side = keys.shape[1] // (2 * d * STEP_HEADS)
    slim, wide = STEP_HEADS * d, 2 * STEP_HEADS * d

    def mine(h, side_ref, code_ref):
        return 0, side_ref[0] * per_side + first // STEP_HEADS + h

    def here(h, side_ref, code_ref):
        return 0, h

    def out(rows, width, dtype):
        return (
            jax.ShapeDtypeStruct((rows, steps * width), dtype),
            pl.BlockSpec((rows, width), here),
        )

    outs = [
        out(n, wide, jnp.bfloat16),
        out(n, wide, jnp.bfloat16),
        out(2 * n, slim, jnp.float32),
        out(2 * n, slim, jnp.float32),
        out(2 * n, slim, jnp.bfloat16),
        out(2 * n, slim, jnp.bfloat16),
        out(2 * n, slim, jnp.bfloat16),
        out(2 * n, slim, jnp.bfloat16),
    ]
    work = [
        pltpu.VMEM((4 * n, d), jnp.bfloat16),
        pltpu.VMEM((4 * n, d), jnp.bfloat16),
        pltpu.VMEM((6 * n, d), jnp.bfloat16),
        pltpu.VMEM((6 * n, d), jnp.bfloat16),
        pltpu.VMEM((6 * n, 2 * n), jnp.float32),
        pltpu.VMEM((6 * n, 2 * n), jnp.float32),
        pltpu.VMEM((6 * n, 4 * n), jnp.bfloat16),
        pltpu.VMEM((6 * n, 4 * n), jnp.bfloat16),
    ]
    return pl.pallas_call(
        attend_kernel,
        grid_spec=pltpu.PrefetchScalarGridSpec(
            num_scalar_prefetch=2,
            grid=(steps,),
            in_specs=[
                pl.BlockSpec((n, wide), mine),
                pl.BlockSpec((n, wide), mine),
                pl.BlockSpec((2 * n, wide), here),
                pl.BlockSpec((n, slim), mine),
                pl.BlockSpec((n, slim), mine),
                pl.BlockSpec((2 * n, slim), here),
                pl.BlockSpec((2 * n, slim), here),
                pl.BlockSpec((2 * n, slim), here),
                pl.BlockSpec((4 * n, slim), here),
            ],
            out_specs=[spec for _, spec in outs],
            scratch_shapes=[pltpu.SMEM((12,), jnp.int32)] + work * STEP_HEADS,
        ),
        out_shape=[shape for shape, _ in outs],
        compiler_params=pltpu.CompilerParams(vmem_limit_bytes=VMEM_BYTES),
    )(side, limits, queries, grads, qg_other, keys, values, kv_other, kv2_own, kv2_other, kv1)


def swap(block):
    return lax.ppermute(block, "space", [(0, 1), (1, 0)])


def mate(block):
    return lax.ppermute(block, "tm", [(i, i ^ 1) for i in range(lax.axis_size("tm"))])


def moved(block, distance):
    size = lax.axis_size("tm")
    return lax.ppermute(
        block, "tm", [(i, i + distance) for i in range(size) if 0 <= i + distance < size]
    )


def after(arrays, *earlier):
    arrays = list(arrays)
    return lax.optimization_barrier((*arrays, *earlier))[: len(arrays)]


def pair_body(queries, keys, values, output_gradient, tiles, kinds):
    n, d = BLOCK_TOKENS, HEAD_SIZE
    side = lax.axis_index("space")
    odd = lax.axis_index("tm") % 2 == 1
    half = keys.shape[1] // (2 * d)
    sizes = [half // 2, half - half // 2]
    firsts = [0, half // 2]
    place = side.reshape(1).astype(jnp.int32)
    codes = 4 * tiles + kinds
    limits = jnp.concatenate([codes[0], codes[1]])

    def kv_part(part, c, *earlier):
        return packed(after([keys, values], *earlier), part, firsts[c] * d, sizes[c] * d)

    def qg_part(part, c, *earlier):
        arrays = after([queries, output_gradient], *earlier)
        return packed(arrays, part, 2 * firsts[c] * d, 2 * sizes[c] * d)

    kv_away = [kv_part(1 - side, 0)]
    kv_away.append(kv_part(1 - side, 1, kv_away[0]))
    kv_own = [kv_part(side, 0, kv_away[1])]
    qg_away = [qg_part(1 - side, 0, kv_own[0])]
    qg_away.append(qg_part(1 - side, 1, qg_away[0]))
    kv_own.append(kv_part(side, 1, qg_away[1]))

    kv_other = [swap(b) for b in kv_away]
    qg_other = [swap(b) for b in qg_away]
    kv2_own, kv2_other = [moved(kv_own[0], 2)], [moved(kv_other[0], 2)]
    late = moved(jnp.concatenate([kv_own[1], kv_other[1]], axis=0), 2)
    kv2_own.append(late[: 2 * n])
    kv2_other.append(late[2 * n :])

    def attended(c, *earlier):
        if earlier:
            kv2_own[c], kv2_other[c] = after([kv2_own[c], kv2_other[c]], e1_own, e1_other)
        kv1 = mate(
            jnp.concatenate(
                [
                    jnp.where(odd, kv2_own[c], kv_own[c]),
                    jnp.where(odd, kv2_other[c], kv_other[c]),
                ],
                axis=0,
            )
        )
        return attend(
            place, after([limits], *earlier)[0] if earlier else limits, firsts[c], sizes[c],
            queries, output_gradient, keys, values,
            qg_other[c], kv_other[c], kv2_own[c], kv2_other[c], kv1,
        )

    def low(total):
        return total.astype(jnp.bfloat16)

    def back_sum(own, met):
        return low(own + jnp.where(odd, met.astype(jnp.float32), 0.0))

    def here_sum(own, met, back):
        return low(own + jnp.where(odd, 0.0, met.astype(jnp.float32)) + back)

    dq_own0, dq_away0, e0_own, e0_other, e1_own, e1_other, e2_own, e2_other = attended(0)
    e1_own, e1_other = after([e1_own, e1_other], qg_other[1])
    dq_other0 = swap(dq_away0)
    e1_own, e1_other = mate(e1_own), mate(e1_other)
    ship0 = [jnp.concatenate([back_sum(e2_own, e1_own), back_sum(e2_other, e1_other)], axis=0)]
    back0 = moved(ship0[0], -2)
    back_own0, back_other0 = back0[: 2 * n], back0[2 * n :]

    dq_own1, dq_away1, d0_own, d0_other, d1_own, d1_other, d2_own, d2_other = attended(1, *ship0)
    dq_other1 = swap(dq_away1)
    d1_other = mate(d1_other)
    d1_own = mate(d1_own)
    d1_other, back_other0 = after([d1_other, back_other0])
    ship_other = back_sum(d2_other, d1_other)
    back_other = moved(ship_other, -2)
    ship_own = back_sum(d2_own, d1_own)
    back_own = moved(ship_own, -2)
    (back_other0,) = after([back_other0], ship_other)
    other0 = swap(here_sum(e0_other, e1_other, back_other0))
    other1 = swap(here_sum(d0_other, d1_other, back_other))
    own0 = here_sum(e0_own, e1_own, back_own0)
    own1 = here_sum(d0_own, d1_own, back_own)

    def placed(own, other):
        own, other = jnp.concatenate(own, axis=1), jnp.concatenate(other, axis=1)
        return jnp.where(
            side == 0,
            jnp.concatenate([own, other], axis=1),
            jnp.concatenate([other, own], axis=1),
        )

    dq_own0, dq_own1, dq_other0, dq_other1 = after(
        [dq_own0, dq_own1, dq_other0, dq_other1], ship_other, ship_own
    )
    grad_queries = placed([dq_own0, dq_own1], [dq_other0, dq_other1])
    blank = jnp.zeros_like(own1[:n])
    grad_keys = placed([own0[:n], own1[:n]], [other0[:n], blank])
    grad_values = placed([own0[n:], own1[n:]], [other0[n:], blank])
    grad_keys, grad_values, other1 = after([grad_keys, grad_values, other1])
    last = ((1 - side) * half + firsts[1]) * d
    return (
        grad_queries,
        lax.dynamic_update_slice_in_dim(grad_keys, other1[:n], last, 1),
        lax.dynamic_update_slice_in_dim(grad_values, other1[n:], last, 1),
    )


def body(queries, keys, values, output_gradient, tiles, kinds):
    pair = (
        lax.axis_size("space") == 2
        and lax.axis_size("tm") % 2 == 0
        and tiles.shape[0] == 2
        and queries.shape[0] == BLOCK_TOKENS
        and queries.shape[1] == 2 * keys.shape[1]
        and keys.shape[1] % (4 * STEP_HEADS * HEAD_SIZE) == 0
    )
    run = pair_body if pair else general_body
    return run(queries, keys, values, output_gradient, tiles, kinds)


def solution(mesh):
    in_specs = (
        P(("tm", "space"), None),
        P(("tm", "space"), None),
        P(("tm", "space"), None),
        P(("tm", "space"), None),
        P("tm", None),
        P("tm", None),
    )
    out_specs = (P(("tm", "space"), None), P(("tm", "space"), None), P(("tm", "space"), None))
    return jax.shard_map(body, mesh=mesh, in_specs=in_specs, out_specs=out_specs, check_vma=False)
```

```python
import math

import jax
import jax.numpy as jnp
from jax import lax
from jax.experimental import pallas as pl
from jax.experimental.pallas import tpu as pltpu
from jax.sharding import PartitionSpec as P

HEAD_SIZE = 128
BLOCK_TOKENS = 128
MAXT = 6
REACH = 2
STEP_HEADS = 1
HIDDEN = -1e30
FAR = 1 << 20
VMEM_BYTES = 53248 * 1024


def shifted_2(block, axis, distance):
    devices = range(lax.axis_size(axis))
    route = [(i - distance, i) for i in devices if i - distance in devices]
    return lax.ppermute(block, axis, route)


def block_grads(query_rows, grad_rows, key_tiles, value_tiles, tile_kinds):
    blocks, length, kv_count, head_dim = key_tiles.shape
    score_scale = 1.0 / head_dim**0.5
    key_flat = key_tiles.reshape(blocks * length, kv_count, head_dim)
    value_flat = value_tiles.reshape(blocks * length, kv_count, head_dim)
    scores = (
        jnp.einsum("qkgd,tkd->kgqt", query_rows, key_flat, preferred_element_type=jnp.float32)
        * score_scale
    )
    query_pos = jnp.arange(length)
    column_kind = jnp.repeat(tile_kinds, length)
    column_pos = jnp.tile(jnp.arange(length), blocks)
    visible = (column_kind == 0)[None, :] | (column_kind == 1)[None, :] & (
        column_pos[None, :] <= query_pos[:, None]
    )
    masked = jnp.where(visible, scores, -jnp.inf)
    row_max = jnp.max(masked, axis=-1, keepdims=True)
    weights = jnp.where(visible, jnp.exp(masked - row_max), 0.0)
    probabilities = weights / jnp.sum(weights, axis=-1, keepdims=True)
    probs_low = probabilities.astype(jnp.bfloat16)
    outputs = jnp.einsum(
        "kgqt,tkd->qkgd", probs_low, value_flat, preferred_element_type=jnp.float32
    )
    row_delta = jnp.einsum("qkgd,qkgd->kgq", grad_rows.astype(jnp.float32), outputs)
    grad_probs = jnp.einsum(
        "qkgd,tkd->kgqt", grad_rows, value_flat, preferred_element_type=jnp.float32
    )
    grad_scores = (score_scale * probabilities * (grad_probs - row_delta[..., None])).astype(
        jnp.bfloat16
    )
    grad_query = jnp.einsum(
        "kgqt,tkd->qkgd", grad_scores, key_flat, preferred_element_type=jnp.float32
    )
    grad_key = jnp.einsum(
        "kgqt,qkgd->tkd", grad_scores, query_rows, preferred_element_type=jnp.float32
    )
    grad_value = jnp.einsum(
        "kgqt,qkgd->tkd", probs_low, grad_rows, preferred_element_type=jnp.float32
    )
    return (
        grad_query.astype(jnp.bfloat16),
        grad_key.reshape(blocks, length, kv_count, head_dim),
        grad_value.reshape(blocks, length, kv_count, head_dim),
    )


def general_body(queries, keys, values, output_gradient, tiles, kinds):
    query_heads, grad_heads, key_heads, value_heads = (
        lax.all_to_all(queries, "space", split_axis=1, concat_axis=0, tiled=True),
        lax.all_to_all(output_gradient, "space", split_axis=1, concat_axis=0, tiled=True),
        lax.all_to_all(keys, "space", split_axis=1, concat_axis=0, tiled=True),
        lax.all_to_all(values, "space", split_axis=1, concat_axis=0, tiled=True),
    )
    window = query_heads.shape[0]
    kv_heads = key_heads.shape[1] // HEAD_SIZE
    head_groups = query_heads.shape[1] // key_heads.shape[1]
    per_window = window // BLOCK_TOKENS
    earlier = [shifted_2((key_heads, value_heads), "tm", offset) for offset in range(1, REACH + 1)]
    tile_count = (REACH + 1) * per_window
    key_tiles = jnp.concatenate([key_heads] + [shifted[0] for shifted in earlier], axis=0)
    key_tiles = key_tiles.reshape(tile_count, BLOCK_TOKENS, kv_heads, HEAD_SIZE)
    value_tiles = jnp.concatenate([value_heads] + [shifted[1] for shifted in earlier], axis=0)
    value_tiles = value_tiles.reshape(tile_count, BLOCK_TOKENS, kv_heads, HEAD_SIZE)
    group_size = math.gcd(per_window, 4)
    rounds = per_window // group_size
    query_groups = query_heads.reshape(
        rounds, group_size, BLOCK_TOKENS, kv_heads, head_groups, HEAD_SIZE
    )
    grad_groups = grad_heads.reshape(
        rounds, group_size, BLOCK_TOKENS, kv_heads, head_groups, HEAD_SIZE
    )
    tile_groups = tiles.reshape(rounds, group_size, MAXT)
    kind_groups = kinds.reshape(rounds, group_size, MAXT)

    def one_round(totals, inputs):
        summed_key_grad, summed_value_grad = totals
        query_part, grad_part, tile_part, kind_part = inputs
        flat_tiles = tile_part.reshape(group_size * MAXT)
        grad_query, grad_key, grad_value = jax.vmap(block_grads)(
            query_part, grad_part, key_tiles[tile_part], value_tiles[tile_part], kind_part
        )
        summed_key_grad = summed_key_grad.at[flat_tiles].add(
            grad_key.reshape(group_size * MAXT, BLOCK_TOKENS, kv_heads, HEAD_SIZE)
        )
        summed_value_grad = summed_value_grad.at[flat_tiles].add(
            grad_value.reshape(group_size * MAXT, BLOCK_TOKENS, kv_heads, HEAD_SIZE)
        )
        return ((summed_key_grad, summed_value_grad), grad_query)

    blank_total_sum = jnp.zeros((tile_count, BLOCK_TOKENS, kv_heads, HEAD_SIZE), jnp.float32)
    (summed_key_grad, summed_value_grad), grad_queries = lax.scan(
        one_round,
        (blank_total_sum, blank_total_sum),
        (query_groups, grad_groups, tile_groups, kind_groups),
    )
    key_parts = summed_key_grad.reshape(REACH + 1, window, kv_heads * HEAD_SIZE)
    value_parts = summed_value_grad.reshape(REACH + 1, window, kv_heads * HEAD_SIZE)
    moving_sum = (key_parts[REACH], value_parts[REACH])
    for offset in range(REACH - 1, -1, -1):
        arrived = shifted_2((moving_sum[0], moving_sum[1]), "tm", -1)
        moving_sum = (arrived[0] + key_parts[offset], arrived[1] + value_parts[offset])
    key_total, value_total = moving_sum
    grad_query_heads = grad_queries.reshape(window, head_groups * kv_heads * HEAD_SIZE)
    return (
        lax.all_to_all(grad_query_heads, "space", split_axis=0, concat_axis=1, tiled=True),
        lax.all_to_all(
            key_total.astype(jnp.bfloat16), "space", split_axis=0, concat_axis=1, tiled=True
        ),
        lax.all_to_all(
            value_total.astype(jnp.bfloat16), "space", split_axis=0, concat_axis=1, tiled=True
        ),
    )


def packed(arrays, half, first, width):
    start = half * (arrays[0].shape[1] // 2) + first
    return jnp.concatenate([lax.dynamic_slice_in_dim(a, start, width, 1) for a in arrays], axis=0)


def dot(a, b, contract):
    return lax.dot_general(a, b, ((contract[:1], contract[1:]), ((), ())), preferred_element_type=jnp.float32)


def find_limits(side, code_ref, limit_ref):
    for r in range(2):
        block = side if r == 0 else 1 - side
        codes = [code_ref[block * MAXT + m] for m in range(MAXT)]
        for p in range(2 * (REACH + 1)):
            value = p // 2 * 2 + (side if p % 2 == 0 else 1 - side)
            limit = -FAR
            for code in codes:
                limit = jnp.where(code == 4 * value, FAR, jnp.where(code == 4 * value + 1, 0, limit))
            limit_ref[r * 6 + p] = limit


def attend_kernel(
    side_ref, code_ref,
    q_own, g_own, qg_other, k_own, v_own, kv_other, kv2_own, kv2_other, kv1,
    dq_own, dq_other, d0_own, d0_other, d1_own, d1_other, d2_own, d2_other,
    limit_ref, *scratch,
):
    n, d = BLOCK_TOKENS, HEAD_SIZE

    @pl.when(pl.program_id(0) == 0)
    def _():
        find_limits(side_ref[0], code_ref, limit_ref)

    lanes = 2 * n
    column = lax.broadcasted_iota(jnp.int32, (n, lanes), 0)
    row = lax.broadcasted_iota(jnp.int32, (n, lanes), 1)
    ahead = column - jnp.where(row >= n, row - n, row)
    scale = 1.0 / math.sqrt(d)
    rate = scale * math.log2(math.e)
    for h in range(STEP_HEADS):
        q_all, g_all, k_all, v_all, s_ref, dp_ref, p_ref, ds_ref = scratch[8 * h : 8 * h + 8]
        wide, slim = slice(2 * h * d, 2 * (h + 1) * d), slice(h * d, (h + 1) * d)
        for r, (q, g) in enumerate(
            ((q_own[:, wide], g_own[:, wide]), (qg_other[:n, wide], qg_other[n:, wide]))
        ):
            for j in range(2):
                rows = slice((2 * r + j) * n, (2 * r + j + 1) * n)
                q_all[rows, :] = q[:, j * d : (j + 1) * d]
                g_all[rows, :] = g[:, j * d : (j + 1) * d]
        tiles = (
            (k_own[:, slim], v_own[:, slim]),
            (kv_other[:n, slim], kv_other[n:, slim]),
            (kv1[:n, slim], kv1[n : 2 * n, slim]),
            (kv1[2 * n : 3 * n, slim], kv1[3 * n :, slim]),
            (kv2_own[:n, slim], kv2_own[n:, slim]),
            (kv2_other[:n, slim], kv2_other[n:, slim]),
        )
        for p, (k, v) in enumerate(tiles):
            k_all[p * n : (p + 1) * n, :] = k
            v_all[p * n : (p + 1) * n, :] = v
        for r in range(2):
            cols = slice(r * lanes, (r + 1) * lanes)
            q, g = q_all[cols, :], g_all[cols, :]
            top = None
            for p in range(6):
                rows = slice(p * n, (p + 1) * n)
                s = dot(k_all[rows, :], q, (1, 1))
                s = jnp.where(ahead <= limit_ref[r * 6 + p], s, HIDDEN)
                s_ref[rows, :] = s
                high = jnp.max(s.reshape(n // 8, 8, lanes), axis=0)
                top = high if top is None else jnp.maximum(top, high)
            top = jnp.max(top, axis=0, keepdims=True)
            total = jnp.zeros((8, lanes), jnp.float32)
            delta = jnp.zeros((8, lanes), jnp.float32)
            for p in range(6):
                rows = slice(p * n, (p + 1) * n)
                e = jnp.exp2((s_ref[rows, :] - top) * rate)
                dp = dot(v_all[rows, :], g, (1, 1))
                s_ref[rows, :] = e
                dp_ref[rows, :] = dp
                total = total + jnp.sum(e.reshape(n // 8, 8, lanes), axis=0)
                delta = delta + jnp.sum((e * dp).reshape(n // 8, 8, lanes), axis=0)
            share = 1.0 / jnp.sum(total, axis=0, keepdims=True)
            delta = jnp.sum(delta, axis=0, keepdims=True) * share
            for p in range(6):
                rows = slice(p * n, (p + 1) * n)
                prob = s_ref[rows, :] * share
                ds = prob * (dp_ref[rows, :] - delta)
                p_ref[rows, cols] = prob.astype(jnp.bfloat16)
                ds_ref[rows, cols] = ds.astype(jnp.bfloat16)
        dk = dot(ds_ref[...], q_all[...], (1, 0)) * scale
        dv = dot(p_ref[...], g_all[...], (1, 0))
        for p, out in enumerate((d0_own, d0_other, d1_own, d1_other, d2_own, d2_other)):
            rows = slice(p * n, (p + 1) * n)
            out[:n, slim] = dk[rows].astype(out.dtype)
            out[n:, slim] = dv[rows].astype(out.dtype)
        dq = (dot(k_all[...], ds_ref[...], (0, 0)) * scale).T.astype(jnp.bfloat16)
        for j in range(2):
            here = slice((2 * h + j) * d, (2 * h + j + 1) * d)
            dq_own[:, here] = dq[j * n : (j + 1) * n, :]
            dq_other[:, here] = dq[(2 + j) * n : (3 + j) * n, :]


def attend(side, limits, first, heads, queries, grads, keys, values, qg_other, kv_other, kv2_own, kv2_other, kv1):
    n, d = BLOCK_TOKENS, HEAD_SIZE
    steps = heads // STEP_HEADS
    per_side = keys.shape[1] // (2 * d * STEP_HEADS)
    slim, wide = STEP_HEADS * d, 2 * STEP_HEADS * d

    def mine(h, side_ref, code_ref):
        return 0, side_ref[0] * per_side + first // STEP_HEADS + h

    def here(h, side_ref, code_ref):
        return 0, h

    def out(rows, width, dtype):
        return (
            jax.ShapeDtypeStruct((rows, steps * width), dtype),
            pl.BlockSpec((rows, width), here),
        )

    outs = [
        out(n, wide, jnp.bfloat16),
        out(n, wide, jnp.bfloat16),
        out(2 * n, slim, jnp.float32),
        out(2 * n, slim, jnp.float32),
        out(2 * n, slim, jnp.bfloat16),
        out(2 * n, slim, jnp.bfloat16),
        out(2 * n, slim, jnp.bfloat16),
        out(2 * n, slim, jnp.bfloat16),
    ]
    work = [
        pltpu.VMEM((4 * n, d), jnp.bfloat16),
        pltpu.VMEM((4 * n, d), jnp.bfloat16),
        pltpu.VMEM((6 * n, d), jnp.bfloat16),
        pltpu.VMEM((6 * n, d), jnp.bfloat16),
        pltpu.VMEM((6 * n, 2 * n), jnp.float32),
        pltpu.VMEM((6 * n, 2 * n), jnp.float32),
        pltpu.VMEM((6 * n, 4 * n), jnp.bfloat16),
        pltpu.VMEM((6 * n, 4 * n), jnp.bfloat16),
    ]
    return pl.pallas_call(
        attend_kernel,
        grid_spec=pltpu.PrefetchScalarGridSpec(
            num_scalar_prefetch=2,
            grid=(steps,),
            in_specs=[
                pl.BlockSpec((n, wide), mine),
                pl.BlockSpec((n, wide), mine),
                pl.BlockSpec((2 * n, wide), here),
                pl.BlockSpec((n, slim), mine),
                pl.BlockSpec((n, slim), mine),
                pl.BlockSpec((2 * n, slim), here),
                pl.BlockSpec((2 * n, slim), here),
                pl.BlockSpec((2 * n, slim), here),
                pl.BlockSpec((4 * n, slim), here),
            ],
            out_specs=[spec for _, spec in outs],
            scratch_shapes=[pltpu.SMEM((12,), jnp.int32)] + work * STEP_HEADS,
        ),
        out_shape=[shape for shape, _ in outs],
        compiler_params=pltpu.CompilerParams(vmem_limit_bytes=VMEM_BYTES),
    )(side, limits, queries, grads, qg_other, keys, values, kv_other, kv2_own, kv2_other, kv1)


def swap(block):
    return lax.ppermute(block, "space", [(0, 1), (1, 0)])


def mate(block):
    return lax.ppermute(block, "tm", [(i, i ^ 1) for i in range(lax.axis_size("tm"))])


def moved(block, distance):
    size = lax.axis_size("tm")
    return lax.ppermute(
        block, "tm", [(i, i + distance) for i in range(size) if 0 <= i + distance < size]
    )


def after(arrays, *earlier):
    arrays = list(arrays)
    return lax.optimization_barrier((*arrays, *earlier))[: len(arrays)]


def pair_body(queries, keys, values, output_gradient, tiles, kinds):
    n, d = BLOCK_TOKENS, HEAD_SIZE
    side = lax.axis_index("space")
    odd = lax.axis_index("tm") % 2 == 1
    half = keys.shape[1] // (2 * d)
    sizes = [half // 2, half - half // 2]
    firsts = [0, half // 2]
    place = side.reshape(1).astype(jnp.int32)
    codes = 4 * tiles + kinds
    limits = jnp.concatenate([codes[0], codes[1]])

    def kv_part(part, c, *earlier):
        return packed(after([keys, values], *earlier), part, firsts[c] * d, sizes[c] * d)

    def qg_part(part, c, *earlier):
        arrays = after([queries, output_gradient], *earlier)
        return packed(arrays, part, 2 * firsts[c] * d, 2 * sizes[c] * d)

    kv_away = [kv_part(1 - side, 0)]
    kv_away.append(kv_part(1 - side, 1, kv_away[0]))
    kv_own = [kv_part(side, 0, kv_away[1])]
    qg_away = [qg_part(1 - side, 0, kv_own[0])]
    qg_away.append(qg_part(1 - side, 1, qg_away[0]))
    kv_own.append(kv_part(side, 1, qg_away[1]))

    kv_other = [swap(b) for b in kv_away]
    qg_other = [swap(b) for b in qg_away]
    kv2_own, kv2_other = [moved(kv_own[0], 2)], [moved(kv_other[0], 2)]
    late = moved(jnp.concatenate([kv_own[1], kv_other[1]], axis=0), 2)
    kv2_own.append(late[: 2 * n])
    kv2_other.append(late[2 * n :])

    def attended(c, *earlier):
        if earlier:
            kv2_own[c], kv2_other[c] = after([kv2_own[c], kv2_other[c]], e1_own, e1_other)
        kv1 = mate(
            jnp.concatenate(
                [
                    jnp.where(odd, kv2_own[c], kv_own[c]),
                    jnp.where(odd, kv2_other[c], kv_other[c]),
                ],
                axis=0,
            )
        )
        return attend(
            place, after([limits], *earlier)[0] if earlier else limits, firsts[c], sizes[c],
            queries, output_gradient, keys, values,
            qg_other[c], kv_other[c], kv2_own[c], kv2_other[c], kv1,
        )

    def low(total):
        return total.astype(jnp.bfloat16)

    def back_sum(own, met):
        return low(own + jnp.where(odd, met.astype(jnp.float32), 0.0))

    def here_sum(own, met, back):
        return low(own + jnp.where(odd, 0.0, met.astype(jnp.float32)) + back)

    dq_own0, dq_away0, e0_own, e0_other, e1_own, e1_other, e2_own, e2_other = attended(0)
    e1_own, e1_other = after([e1_own, e1_other], qg_other[1])
    e1_own, e1_other = after([e1_own, e1_other], late)
    dq_other0 = swap(dq_away0)
    e1_own, e1_other = mate(e1_own), mate(e1_other)
    ship0 = [jnp.concatenate([back_sum(e2_own, e1_own), back_sum(e2_other, e1_other)], axis=0)]
    back0 = moved(ship0[0], -2)
    back_own0, back_other0 = back0[: 2 * n], back0[2 * n :]

    dq_own1, dq_away1, d0_own, d0_other, d1_own, d1_other, d2_own, d2_other = attended(1, *ship0)
    dq_other1 = swap(dq_away1)
    d1_other = mate(d1_other)
    d1_own = mate(d1_own)
    d1_other, back_other0 = after([d1_other, back_other0])
    ship_other = back_sum(d2_other, d1_other)
    back_other = moved(ship_other, -2)
    ship_own = back_sum(d2_own, d1_own)
    back_own = moved(ship_own, -2)
    (back_other0,) = after([back_other0], ship_other)
    other0 = swap(here_sum(e0_other, e1_other, back_other0))
    other1 = swap(here_sum(d0_other, d1_other, back_other))
    own0 = here_sum(e0_own, e1_own, back_own0)
    own1 = here_sum(d0_own, d1_own, back_own)

    def placed(own, other):
        own, other = jnp.concatenate(own, axis=1), jnp.concatenate(other, axis=1)
        return jnp.where(
            side == 0,
            jnp.concatenate([own, other], axis=1),
            jnp.concatenate([other, own], axis=1),
        )

    dq_own0, dq_own1, dq_other0, dq_other1 = after(
        [dq_own0, dq_own1, dq_other0, dq_other1], ship_other, ship_own
    )
    grad_queries = placed([dq_own0, dq_own1], [dq_other0, dq_other1])
    blank = jnp.zeros_like(own1[:n])
    grad_keys = placed([own0[:n], own1[:n]], [other0[:n], blank])
    grad_values = placed([own0[n:], own1[n:]], [other0[n:], blank])
    grad_keys, grad_values, other1 = after([grad_keys, grad_values, other1])
    last = ((1 - side) * half + firsts[1]) * d
    return (
        grad_queries,
        lax.dynamic_update_slice_in_dim(grad_keys, other1[:n], last, 1),
        lax.dynamic_update_slice_in_dim(grad_values, other1[n:], last, 1),
    )


def body(queries, keys, values, output_gradient, tiles, kinds):
    pair = (
        lax.axis_size("space") == 2
        and lax.axis_size("tm") % 2 == 0
        and tiles.shape[0] == 2
        and queries.shape[0] == BLOCK_TOKENS
        and queries.shape[1] == 2 * keys.shape[1]
        and keys.shape[1] % (4 * HEAD_SIZE) == 0
    )
    run = pair_body if pair else general_body
    return run(queries, keys, values, output_gradient, tiles, kinds)


def solution(mesh):
    in_specs = (
        P(("tm", "space"), None),
        P(("tm", "space"), None),
        P(("tm", "space"), None),
        P(("tm", "space"), None),
        P("tm", None),
        P("tm", None),
    )
    out_specs = (P(("tm", "space"), None), P(("tm", "space"), None), P(("tm", "space"), None))
    return jax.shard_map(body, mesh=mesh, in_specs=in_specs, out_specs=out_specs, check_vma=False)
```
